256 devices in a mesh: seq: 64 (over z, x, core), head: 4 (over y).
Axes of the slice: x: 4, y: 4, z: 8, core: 2. Of those that a mesh axis runs over, the one named last changes fastest.
Arguments:
- queries: bfloat16 [32768, 2048], P(('seq', 'head')), may hold values from -5 to 5
- keys: bfloat16 [32768, 2048], P(('seq', 'head')), may hold values from -5 to 5
- values: bfloat16 [32768, 2048], P(('seq', 'head')), may hold values from -6 to 6
- noise: bfloat16 [32768, 2048], P(('seq', 'head')), may hold values from -6 to 6
- random_blocks: int32 [512, 3], replicated, may hold values from 0 to 511, as said below
- global_blocks: int32 [2], replicated, may hold values from 0 to 511
Outputs:
- attended: bfloat16 [32768, 2048], P(('seq', 'head'))
- query_grad: bfloat16 [32768, 2048], P(('seq', 'head'))
- key_grad: bfloat16 [32768, 2048], P(('seq', 'head'))
- value_grad: bfloat16 [32768, 2048], P(('seq', 'head'))
The draws below stay inside these ranges and needn't reach their ends.
Inputs may be any that keep to these rules, and one draw needn't show every extreme that they name: `random_blocks`: group the blocks into shards of 8 consecutive blocks. No query block names a random block of its own shard, and the 8 query blocks of one shard name together at most 1 random blocks of any one other shard, counting repeats; in every draw some shard names exactly 1 of some other shard.
All inputs are finite; a program needn't handle non-finite values.
Results may differ from the reference program's by a relative error of at most 0.033.
Values may be sent and summed in bfloat16 or wider, within the bound.
A program may use at most 128 MiB of HBM per device.

```python
import math
import jax
import jax.numpy as jnp
from jax import lax

HEADS = 16
DH = 128
BLK = 64
R = 3
G = 2
HW = 2048
QB = 8
NB = 512
TOKENS = 32768


def draw_queries(key, part):
    base = jnp.clip(jax.random.normal(jax.random.fold_in(key, 1), (TOKENS, HW), jnp.float32), -4.5, 4.5)
    return base.astype(jnp.bfloat16)


def draw_keys(key, part):
    base = jnp.clip(jax.random.normal(jax.random.fold_in(key, 2), (TOKENS, HW), jnp.float32), -4.5, 4.5)
    return base.astype(jnp.bfloat16)


def draw_noise(key, part):
    coins = jax.random.bernoulli(jax.random.fold_in(key, 7), 0.5, (TOKENS // BLK, 1, HW))
    shared = jnp.broadcast_to(jnp.where(coins, 1.0, -1.0).astype(jnp.float32), (TOKENS // BLK, BLK, HW)).reshape(TOKENS, HW)
    rough = jnp.clip(jax.random.normal(jax.random.fold_in(key, 8), (TOKENS, HW), jnp.float32), -4.5, 4.5)
    return (shared + rough).astype(jnp.bfloat16)


def draw_random_blocks(key, part):
    seq_total = NB // QB
    requests = QB * R

    def one_seq(position):
        seq_key = jax.random.fold_in(key, position)
        owner_order = jax.random.permutation(jax.random.fold_in(seq_key, 1), seq_total - 1).astype(jnp.int32)
        picked = owner_order[jnp.arange(requests, dtype=jnp.int32) % (seq_total - 1)]
        owner_seq = picked + (picked >= position).astype(jnp.int32)
        inner_blk = jax.random.randint(jax.random.fold_in(seq_key, 2), (requests,), 0, QB, jnp.int32)
        chosen = owner_seq * QB + inner_blk
        shuffle = jax.random.permutation(jax.random.fold_in(seq_key, 3), requests)
        return chosen[shuffle]
    all_rows = jax.vmap(one_seq)(jnp.arange(seq_total, dtype=jnp.int32))
    return all_rows.reshape(NB, R).astype(jnp.int32)


def shard_levels(rng, dims, cuts, least, high):
    loudness, own = 1.0, jax.random.fold_in(rng, 6)
    for axis_at, parts in cuts:
        heights = jnp.exp(jax.random.uniform(jax.random.fold_in(own, axis_at), (parts,), jnp.float32, least / len(cuts), high / len(cuts)))
        loudness = loudness * jnp.repeat(heights, dims[axis_at] // parts).reshape([-1 if axis == axis_at else 1 for axis in range(len(dims))])
    return loudness


def gaussian(key, shape, scale, limit, shards=(), kind=jnp.bfloat16):
    loudness = shard_levels(key, shape, shards, -0.22, 0.18) if shards else 1.0
    result = jax.random.normal(key, shape, jnp.float32) * scale * loudness
    return jnp.minimum(jnp.maximum(result, -limit), limit).astype(kind)


def setup_inputs(seed: int = 0) -> dict:
    arg_keys = jax.random.split(jax.random.key(seed), 7)
    queries = draw_queries(jax.random.fold_in(arg_keys[6], 71), 0)
    keys = draw_keys(jax.random.fold_in(arg_keys[6], 71), 0)
    values = gaussian(arg_keys[2], (TOKENS, HW), 1.0, 6.0, ((0, 256),))
    noise = draw_noise(jax.random.fold_in(arg_keys[6], 71), 0)
    random_blocks = draw_random_blocks(jax.random.fold_in(arg_keys[6], 71), 0)
    global_blocks = jax.random.randint(arg_keys[5], (G,), 0, NB).astype(jnp.int32)
    return {"queries": queries, "keys": keys, "values": values, "noise": noise, "random_blocks": random_blocks, "global_blocks": global_blocks}


def settle(value):
    return lax.optimization_barrier(value.astype(jnp.bfloat16)).astype(jnp.float32)

def reference(queries, keys, values, noise, random_blocks, global_blocks):
    scaling = 1.0 / math.sqrt(DH)
    block_total = NB
    key_count = 3 + R + G
    query_four = queries.reshape(block_total, BLK, HEADS, DH)
    key_four = keys.reshape(block_total, BLK, HEADS, DH)
    value_four = values.reshape(block_total, BLK, HEADS, DH)
    noise_four = noise.reshape(block_total, BLK, HEADS, DH)
    block_ids = jnp.arange(block_total, dtype=jnp.int32)
    key_lists = jnp.concatenate([(block_ids - 1)[:, None], block_ids[:, None], (block_ids + 1)[:, None], random_blocks.astype(jnp.int32), jnp.broadcast_to(global_blocks.astype(jnp.int32)[None, :], (block_total, G))], axis=1)
    present = jnp.concatenate([(block_ids >= 1)[:, None], jnp.ones((block_total, 1), jnp.bool_), (block_ids + 1 < block_total)[:, None], jnp.ones((block_total, R + G), jnp.bool_)], axis=1)
    key_lists = jnp.clip(key_lists, 0, block_total - 1).astype(jnp.int32)
    random_cols = (jnp.arange(key_count) >= 3) & (jnp.arange(key_count) < 3 + R)

    def group_step(accum, group_idx):
        key_acc, value_acc = accum
        first_blk = (group_idx * QB).astype(jnp.int32)
        group_q = lax.dynamic_slice_in_dim(query_four, first_blk, QB, 0).astype(jnp.float32)
        group_noise = lax.dynamic_slice_in_dim(noise_four, first_blk, QB, 0).astype(jnp.float32)
        group_lists = lax.dynamic_slice_in_dim(key_lists, first_blk, QB, 0)
        group_present = lax.dynamic_slice_in_dim(present, first_blk, QB, 0)
        group_k = key_four[group_lists].astype(jnp.float32)
        group_v = value_four[group_lists].astype(jnp.float32)
        scores = jnp.einsum('iahd,ijbhd->ihajb', group_q, group_k) * scaling
        scores = jnp.where(group_present[:, None, None, :, None], scores, -jnp.inf)
        row_max = lax.optimization_barrier(jnp.max(scores, axis=(3, 4), keepdims=True))
        weights_raw = jnp.exp(scores - row_max)
        probs_full = weights_raw / lax.optimization_barrier(jnp.sum(weights_raw, axis=(3, 4), keepdims=True))
        probs_bf = settle(probs_full)
        attended = jnp.einsum('ihajb,ijbhd->iahd', probs_bf, group_v).astype(jnp.bfloat16)
        out_grad = settle(attended.astype(jnp.float32) - group_noise)
        dprobs = jnp.einsum('iahd,ijbhd->ihajb', out_grad, group_v)
        delta_row = lax.optimization_barrier(jnp.sum(probs_full * dprobs, axis=(3, 4), keepdims=True))
        dscores = settle(probs_full * (dprobs - delta_row))
        query_grad = (jnp.einsum('ihajb,ijbhd->iahd', dscores, group_k) * scaling).astype(jnp.bfloat16)
        key_terms = jnp.einsum('ihajb,iahd->ijbhd', dscores, group_q) * scaling
        value_terms = jnp.einsum('ihajb,iahd->ijbhd', probs_bf, out_grad)
        chosen = random_cols[None, :, None, None, None]
        key_terms = jnp.where(chosen, settle(key_terms), key_terms)
        value_terms = jnp.where(chosen, settle(value_terms), value_terms)
        flat_lists = group_lists.reshape(-1)
        key_acc = key_acc.at[flat_lists].add(key_terms.reshape(QB * key_count, BLK, HEADS, DH))
        value_acc = value_acc.at[flat_lists].add(value_terms.reshape(QB * key_count, BLK, HEADS, DH))
        return ((key_acc, value_acc), (attended, query_grad))
    zeros_acc = jnp.zeros((block_total, BLK, HEADS, DH), jnp.float32)
    group_ids = jnp.arange(block_total // QB, dtype=jnp.int32)
    (key_acc, value_acc), (attended, query_grad) = lax.scan(group_step, (zeros_acc, zeros_acc), group_ids)
    attended = attended.reshape(TOKENS, HW)
    query_grad = query_grad.reshape(TOKENS, HW)
    key_grad = key_acc.reshape(TOKENS, HW).astype(jnp.bfloat16)
    value_grad = value_acc.reshape(TOKENS, HW).astype(jnp.bfloat16)
    return (attended, query_grad, key_grad, value_grad)
```

```python
import functools
import math

import jax
import jax.numpy as jnp
from jax import lax
from jax.experimental import pallas as pl
from jax.experimental.pallas import tpu as pltpu
from jax.sharding import PartitionSpec as P

DH = 128
BLK = 64
NX, NY, NZ, NC = 4, 4, 8, 2
ROWS = 128
SHARD = NY * ROWS
PER = SHARD // BLK
NB = NZ * NX * NC * PER
QUERIES = NX * PER
ENTRIES = 8
GROUP = 4
MESH = pl.DeviceIdType.MESH
STEPS = ((4, 3), (3, 4))


def place():
    seq, y = lax.axis_index("seq"), lax.axis_index("head")
    return seq // (NX * NC), (seq // NC) % NX, y, seq % NC


def device(z, x, y, c):
    return ((z * NX + x) * NC + c, y)


def around(base, step, count):
    return (base + step + count) % count


def greet(z, x, y, c):
    barrier = pltpu.get_barrier_semaphore()

    def signal(target):
        pl.semaphore_signal(barrier, inc=1, device_id=target, device_id_type=MESH)

    def plane(p, carry):
        signal(device(z, (x + p // NY) % NX, (y + p % NY) % NY, c))
        return carry

    lax.fori_loop(1, NX * NY, plane, 0)
    signal(device((z + 1) % NZ, x, y, c))
    signal(device((z + NZ - 1) % NZ, x, y, c))
    signal(device(z, x, y, 1 - c))
    pl.semaphore_wait(barrier, NX * NY - 1 + 3)


def remote(src, dst, send, recv, target):
    return pltpu.make_async_remote_copy(
        src_ref=src, dst_ref=dst, send_sem=send, recv_sem=recv, device_id=target, device_id_type=MESH
    )


def fetch_kernel(
    q, k, v, n, q_out, n_out, kv,
    plane_send, plane_recv, own_sem, ring_send, ring_recv, pair_send, pair_recv,
):
    z, x, y, c = place()
    greet(z, x, y, c)

    def columns(h):
        return pl.ds(pl.multiple_of(h * DH, DH), DH)

    def rows(at):
        return pl.ds(pl.multiple_of(at * ROWS, ROWS), ROWS)

    def landing(a, xs, ys):
        if a < 2:
            return kv.at[a, z, xs, c, rows(ys)]
        return (q_out, n_out)[a - 2].at[xs, rows(ys)]

    sources = (k, v, q, n)

    def tile_out(a, p):
        px, py = (x + p // NY) % NX, (y + p % NY) % NY
        return remote(
            sources[a].at[:, columns(px * NY + py)], landing(a, x, y),
            plane_send.at[a, p], plane_recv.at[a, p], device(z, px, py, c),
        )

    def tile_in(a, p):
        px, py = (x + NX - p // NY) % NX, (y + NY - p % NY) % NY
        return remote(
            sources[a].at[:, columns(px * NY + py)], landing(a, px, py),
            plane_send.at[a, p], plane_recv.at[a, p], device(z, px, py, c),
        )

    def tile_own(a):
        return pltpu.make_async_copy(
            sources[a].at[:, columns(x * NY + y)], landing(a, x, y), own_sem.at[a]
        )

    for a in range(4):
        tile_own(a).start()
    for first in (0, 2):
        def start(p, carry):
            tile_out(first, p).start()
            tile_out(first + 1, p).start()
            return carry

        lax.fori_loop(1, NX * NY, start, 0)

    def ring(a, way, step, j):
        sign = 1 if way == 0 else -1
        chunk = kv.at[a, around(z, -sign * (step - 1), NZ), around(x, -j, NX), c]
        return remote(
            chunk, chunk, ring_send.at[a, way, step - 1, j], ring_recv.at[a, way, step - 1, j],
            device(around(z, sign, NZ), x, y, c),
        )

    def ring_in(a, way, step, j):
        sign = 1 if way == 0 else -1
        chunk = kv.at[a, around(z, -sign * step, NZ), around(x, -j, NX), c]
        return remote(
            chunk, chunk, ring_send.at[a, way, step - 1, j], ring_recv.at[a, way, step - 1, j],
            device(around(z, -sign, NZ), x, y, c),
        )

    def pair(a, off, j, core):
        chunk = kv.at[a, around(z, off, NZ), around(x, -j, NX), core]
        return remote(
            chunk, chunk, pair_send.at[a, off + 4, j], pair_recv.at[a, off + 4, j],
            device(z, x, y, 1 - c),
        )

    def offsets(a):
        right, left = STEPS[a]
        return range(-right, left + 1)

    for step in range(1, 6):
        def chunk_step(j, carry):
            for a in range(2):
                if step == 1:
                    for dy in range(NY):
                        if dy == 0:
                            @pl.when(j == 0)
                            def _():
                                tile_own(a).wait()

                            @pl.when(j > 0)
                            def _():
                                tile_in(a, j * NY).wait_recv()
                        else:
                            tile_in(a, j * NY + dy).wait_recv()
                for way in range(2):
                    count = STEPS[a][way]
                    if 1 < step <= count + 1:
                        ring_in(a, way, step - 1, j).wait_recv()
                    if step <= count:
                        ring(a, way, step, j).start()
                    if 1 < step <= count + 1:
                        pair(a, (step - 1) * (-1 if way == 0 else 1), j, c).start()
                if step == 1:
                    pair(a, 0, j, c).start()
            return carry

        lax.fori_loop(0, NX, chunk_step, 0)

    for a in (2, 3):
        tile_own(a).wait()

    def finish_plane(p, carry):
        for a in range(4):
            tile_out(a, p).wait_send()
            if a >= 2:
                tile_in(a, p).wait_recv()
        return carry

    lax.fori_loop(1, NX * NY, finish_plane, 0)

    def finish_chunks(j, carry):
        for a in range(2):
            for way in range(2):
                for step in range(1, STEPS[a][way] + 1):
                    ring(a, way, step, j).wait_send()
            for off in offsets(a):
                pair(a, off, j, c).wait_send()
                pair(a, off, j, 1 - c).wait_recv()
        return carry

    lax.fori_loop(0, NX, finish_chunks, 0)


def attend_kernel(
    lists, firsts, q, n, kv_hbm, att, dq, part, kv, acc, load_sem, store_sem,
):
    scaling = 1.0 / math.sqrt(DH)
    loads = [pltpu.make_async_copy(kv_hbm.at[a], kv.at[a], load_sem.at[a]) for a in range(2)]
    for load in loads:
        load.start()

    def clear(i, carry):
        for a in range(2):
            acc[a, pl.ds(i * 8, 8)] = jnp.zeros((8, BLK, DH), jnp.float32)
        return carry

    lax.fori_loop(0, NB // 8, clear, 0)
    for load in loads:
        load.wait()

    column = lax.broadcasted_iota(jnp.int32, (1, ENTRIES * BLK), 1) // BLK

    def dot(a, b, dims):
        return lax.dot_general(a, b, (dims, ((), ())), preferred_element_type=jnp.float32)

    def group(g, carry):
        ids = [g * GROUP + u for u in range(GROUP)]
        entries = [[lists[i, e] for e in range(ENTRIES)] for i in ids]
        qs = [q[i] for i in ids]
        ks = [jnp.concatenate([kv[0, e] for e in es], 0) for es in entries]
        scores = [dot(a, b, ((1,), (1,))) * scaling for a, b in zip(qs, ks)]
        masked = []
        for i, s in zip(ids, scores):
            block = firsts[i]
            gone = ((column == 0) & (block == 0)) | ((column == 2) & (block == NB - 1))
            masked.append(jnp.where(gone, -jnp.inf, s))
        raws = [jnp.exp(s - jnp.max(s, 1, keepdims=True)) for s in masked]
        probs = [r * (1.0 / jnp.sum(r, 1, keepdims=True)) for r in raws]
        probs_bf = [p.astype(jnp.bfloat16) for p in probs]
        vs = [jnp.concatenate([kv[1, e] for e in es], 0) for es in entries]
        atts = [dot(p, b, ((1,), (0,))).astype(jnp.bfloat16) for p, b in zip(probs_bf, vs)]
        grads = []
        for i, a in zip(ids, atts):
            att[i] = a
            grads.append((a.astype(jnp.float32) - n[i].astype(jnp.float32)).astype(jnp.bfloat16))
        dprobs = [dot(d, b, ((1,), (1,))) for d, b in zip(grads, vs)]
        dscores = [
            (p * (d - jnp.sum(p * d, 1, keepdims=True))).astype(jnp.bfloat16)
            for p, d in zip(probs, dprobs)
        ]
        for i, d, b in zip(ids, dscores, ks):
            dq[i] = (dot(d, b, ((1,), (0,))) * scaling).astype(jnp.bfloat16)
        dks = [dot(d, a, ((0,), (0,))) * scaling for d, a in zip(dscores, qs)]
        dvs = [dot(p, d, ((0,), (0,))) for p, d in zip(probs_bf, grads)]
        for es, dk, dv in zip(entries, dks, dvs):
            for e in range(ENTRIES):
                acc[0, es[e]] += dk[e * BLK : (e + 1) * BLK]
                acc[1, es[e]] += dv[e * BLK : (e + 1) * BLK]
        return carry

    lax.fori_loop(0, QUERIES // GROUP, group, 0)

    def store(a, i):
        span = pl.ds(i * 64, 64)
        return pltpu.make_async_copy(kv.at[a, span], part.at[a, span], store_sem.at[a, i])

    for a in range(2):
        def out(i, carry):
            def cast(s, inner):
                at = pl.ds(i * 64 + s * 8, 8)
                kv[a, at] = acc[a, at].astype(jnp.bfloat16)
                return inner

            lax.fori_loop(0, 8, cast, 0)
            store(a, i).start()
            return carry

        lax.fori_loop(0, NB // 64, out, 0)
    for a in range(2):
        def done(i, carry):
            store(a, i).wait()
            return carry

        lax.fori_loop(0, NB // 64, done, 0)


def return_kernel(
    att, dq, part, att_out, dq_out, dk_out, dv_out,
    own, sib, came, own_sem, pair_send, pair_recv, ring_send, ring_recv,
    plane_send, plane_recv, tile_sem,
):
    z, x, y, c = place()
    greet(z, x, y, c)

    def columns(h):
        return pl.ds(pl.multiple_of(h * DH, DH), DH)

    def rows(at):
        return pl.ds(pl.multiple_of(at * ROWS, ROWS), ROWS)

    def offsets(a):
        right, left = STEPS[a]
        return range(-left, right + 1)

    def load(a, off):
        at = around(z, off, NZ)
        return pltpu.make_async_copy(part.at[a, at, :, c], own.at[a, at], own_sem.at[a, off + 4])

    def pair(a, off):
        at = around(z, off, NZ)
        return remote(
            part.at[a, at, :, 1 - c], sib.at[a, at], pair_send.at[a, off + 4],
            pair_recv.at[a, off + 4], device(z, x, y, 1 - c),
        )

    for a, off in sorted(((a, off) for a in range(2) for off in offsets(a)), key=lambda m: -abs(m[1])):
        load(a, off).start()
        pair(a, off).start()

    outs = (dk_out, dv_out, att_out, dq_out)

    def source(a, xs, ys):
        if a < 2:
            return own.at[a, z, xs, rows(ys)]
        return (att, dq)[a - 2].at[xs, rows(ys)]

    def tile_out(a, p):
        px, py = (x + p // NY) % NX, (y + p % NY) % NY
        return remote(
            source(a, px, py), outs[a].at[:, columns(x * NY + y)],
            plane_send.at[a, p], plane_recv.at[a, p], device(z, px, py, c),
        )

    def tile_in(a, p):
        px, py = (x + NX - p // NY) % NX, (y + NY - p % NY) % NY
        return remote(
            source(a, x, y), outs[a].at[:, columns(px * NY + py)],
            plane_send.at[a, p], plane_recv.at[a, p], device(z, px, py, c),
        )

    def tile_own(a):
        return pltpu.make_async_copy(source(a, x, y), outs[a].at[:, columns(x * NY + y)], tile_sem.at[a])

    for a in (2, 3):
        tile_own(a).start()

    def start(p, carry):
        tile_out(2, p).start()
        tile_out(3, p).start()
        return carry

    lax.fori_loop(1, NX * NY, start, 0)

    def ring(a, way, step, j):
        sign = 1 if way == 0 else -1
        at = around(z, sign * (STEPS[a][way] - step + 1), NZ)
        return remote(
            own.at[a, at, j], came.at[a, way, step - 1, j], ring_send.at[a, way, step - 1, j],
            ring_recv.at[a, way, step - 1, j], device(around(z, sign, NZ), x, y, c),
        )

    def add(a, off, j, arrived):
        at = around(z, off, NZ)
        total = own[a, at, j].astype(jnp.float32) + sib[a, at, j].astype(jnp.float32)
        for way, step in arrived:
            total += came[a, way, step - 1, j].astype(jnp.float32)
        own[a, at, j] = total.astype(jnp.bfloat16)

    for step in range(1, 5):
        for a in range(2):
            for way in range(2):
                if step <= STEPS[a][way]:
                    off = (1 if way == 0 else -1) * (STEPS[a][way] - step + 1)
                    load(a, off).wait()
                    pair(a, off).wait_recv()

        def chunk_step(j, carry):
            for a in range(2):
                for way in range(2):
                    count = STEPS[a][way]
                    if step <= count:
                        off = (1 if way == 0 else -1) * (count - step + 1)
                        if step > 1:
                            ring(a, way, step - 1, j).wait_recv()
                        add(a, off, j, [(way, step - 1)] if step > 1 else [])
                        ring(a, way, step, j).start()
            return carry

        lax.fori_loop(0, NX, chunk_step, 0)

    for a in range(2):
        load(a, 0).wait()
        pair(a, 0).wait_recv()
    for dx in range(NX):
        j = (x + dx) % NX
        for a in range(2):
            for way in range(2):
                ring(a, way, STEPS[a][way], j).wait_recv()
            add(a, 0, j, [(0, STEPS[a][0]), (1, STEPS[a][1])])
            for dy in range(NY):
                if dx == 0 and dy == 0:
                    tile_own(a).start()
                else:
                    tile_out(a, dx * NY + dy).start()

    def finish_plane(p, carry):
        for a in range(4):
            tile_out(a, p).wait_send()
            tile_in(a, p).wait_recv()
        return carry

    lax.fori_loop(1, NX * NY, finish_plane, 0)
    for a in range(4):
        tile_own(a).wait()

    def finish_ring(j, carry):
        for a in range(2):
            for way in range(2):
                for step in range(1, STEPS[a][way] + 1):
                    ring(a, way, step, j).wait_send()
        return carry

    lax.fori_loop(0, NX, finish_ring, 0)
    for a in range(2):
        for off in offsets(a):
            pair(a, off).wait_send()


ANY = pl.BlockSpec(memory_space=pl.ANY)
VMEM = pl.BlockSpec(memory_space=pltpu.VMEM)
SMEM = pl.BlockSpec(memory_space=pltpu.SMEM)
DMA = pltpu.SemaphoreType.DMA


def bf16(*shape):
    return jax.ShapeDtypeStruct(shape, jnp.bfloat16)


def shards(queries, keys, values, noise, random_blocks, global_blocks):
    z, x, y, c = place()
    q_all, n_all, kv = pl.pallas_call(
        fetch_kernel,
        name="fetch",
        out_shape=(bf16(NX, SHARD, DH), bf16(NX, SHARD, DH), bf16(2, NZ, NX, NC, SHARD, DH)),
        in_specs=[ANY] * 4,
        out_specs=(ANY,) * 3,
        scratch_shapes=[
            DMA((4, NX * NY)), DMA((4, NX * NY)), DMA((4,)),
            DMA((2, 2, 4, NX)), DMA((2, 2, 4, NX)), DMA((2, 9, NX)), DMA((2, 9, NX)),
        ],
        compiler_params=pltpu.CompilerParams(collective_id=0, has_side_effects=True),
    )(queries, keys, values, noise)

    mine = lax.dynamic_index_in_dim(random_blocks.reshape(NZ, NX, NC, PER, 3), z, 0, keepdims=False)
    mine = lax.dynamic_index_in_dim(mine, c, 1, keepdims=False).reshape(QUERIES, 3)
    at = jnp.arange(QUERIES, dtype=jnp.int32)
    firsts = ((z * NX + at // PER) * NC + c) * PER + at % PER
    window = jnp.clip(firsts[:, None] + jnp.arange(-1, 2, dtype=jnp.int32)[None], 0, NB - 1)
    lists = jnp.concatenate(
        [window, mine, jnp.broadcast_to(global_blocks[None], (QUERIES, 2))], 1
    ).astype(jnp.int32)

    att, dq, part = pl.pallas_call(
        attend_kernel,
        name="attend",
        out_shape=(bf16(QUERIES, BLK, DH), bf16(QUERIES, BLK, DH), bf16(2, NB, BLK, DH)),
        in_specs=[SMEM, SMEM, VMEM, VMEM, ANY],
        out_specs=(VMEM, VMEM, ANY),
        scratch_shapes=[
            pltpu.VMEM((2, NB, BLK, DH), jnp.bfloat16),
            pltpu.VMEM((2, NB, BLK, DH), jnp.float32),
            DMA((2,)), DMA((2, NB // 64)),
        ],
        compiler_params=pltpu.CompilerParams(vmem_limit_bytes=60 * 2**20),
    )(
        lists, firsts, q_all.reshape(QUERIES, BLK, DH), n_all.reshape(QUERIES, BLK, DH),
        kv.reshape(2, NB, BLK, DH),
    )

    outs = pl.pallas_call(
        return_kernel,
        name="give_back",
        out_shape=(bf16(ROWS, NX * NY * DH),) * 4,
        in_specs=[ANY] * 3,
        out_specs=(ANY,) * 4,
        scratch_shapes=[
            pltpu.VMEM((2, NZ, NX, SHARD, DH), jnp.bfloat16),
            pltpu.VMEM((2, NZ, NX, SHARD, DH), jnp.bfloat16),
            pltpu.VMEM((2, 2, 4, NX, SHARD, DH), jnp.bfloat16),
            DMA((2, 9)), DMA((2, 9)), DMA((2, 9)),
            DMA((2, 2, 4, NX)), DMA((2, 2, 4, NX)),
            DMA((4, NX * NY)), DMA((4, NX * NY)), DMA((4,)),
        ],
        compiler_params=pltpu.CompilerParams(
            collective_id=1, has_side_effects=True, vmem_limit_bytes=40 * 2**20
        ),
    )(
        att.reshape(NX, SHARD, DH), dq.reshape(NX, SHARD, DH),
        part.reshape(2, NZ, NX, NC, SHARD, DH),
    )
    return tuple(outs)


def solution(mesh):
    rows = P(("seq", "head"), None)
    return jax.shard_map(
        shards,
        mesh=mesh,
        in_specs=(rows, rows, rows, rows, P(), P()),
        out_specs=(rows, rows, rows, rows),
        check_vma=False,
    )
```

```python
import math

import jax
import jax.numpy as jnp
from jax import lax
from jax.experimental import pallas as pl
from jax.experimental.pallas import tpu as pltpu
from jax.sharding import PartitionSpec as P

DH = 128
BLK = 64
NX, NY, NZ, NC = 4, 4, 8, 2
ROWS = 128
SIDE = 2 * ROWS
SHARD = NY * ROWS
PER = SHARD // BLK
NB = NZ * NX * NC * PER
QUERIES = NZ * SIDE // BLK
HEADS = 16
ENTRIES = 8
GROUP = 4
PARTS = NZ // 2
MESH = pl.DeviceIdType.MESH


def place():
    seq, y = lax.axis_index("seq"), lax.axis_index("head")
    return seq // (NX * NC), (seq // NC) % NX, y, seq % NC


def device(z, x, y, c):
    return ((z * NX + x) * NC + c, y)


def around(base, step, count):
    return (base + step + count) % count


def offset(slot):
    return (slot + 1) // 2 * (2 * (slot % 2) - 1)


def beside(y):
    return y + 1 - 2 * (y % 2)


def half(y):
    return (y + 1) // 2 % 2


def greet(z, x, y, c):
    barrier = pltpu.get_barrier_semaphore()

    def signal(target):
        pl.semaphore_signal(barrier, inc=1, device_id=target, device_id_type=MESH)

    def plane(dz, carry):
        signal(device((z + dz) % NZ, x, y, c))
        signal(device((z + dz) % NZ, x, beside(y), c))
        return carry

    lax.fori_loop(1, NZ, plane, 0)
    signal(device(z, x, beside(y), c))
    signal(device(z, around(x, 1, NX), y, c))
    signal(device(z, around(x, -1, NX), y, c))
    signal(device(z, x, NY - 1 - y, c))
    signal(device(z, x, y, 1 - c))
    pl.semaphore_wait(barrier, 2 * NZ - 1 + 4)


def remote(src, dst, send, recv, target):
    return pltpu.make_async_remote_copy(
        src_ref=src, dst_ref=dst, send_sem=send, recv_sem=recv, device_id=target, device_id_type=MESH
    )


def columns(h):
    return pl.ds(pl.multiple_of(h * DH, DH), DH)


def rows(at):
    return pl.ds(pl.multiple_of(at * ROWS, ROWS), ROWS)


def far_way(a, part):
    return 1 if (a + part) % 2 == 0 else -1


LONG1, LONG2, SHORT = 0, 1, 2


def fetch_kernel(
    q, k, v, n, q_out, n_out, kv,
    tile_send, tile_recv, own_sem, x_send, x_recv, y_send, y_recv, pair_send, pair_recv,
):
    z, x, y, c = place()
    greet(z, x, y, c)
    side = y // 2
    sources = (k, v, q, n)

    def landing(a, slot, row):
        if a < 2:
            return kv.at[a, slot, x, c, side, rows(row)]
        return (q_out, n_out)[a - 2].at[slot, rows(row)]

    def tile_out(a, slot, turn):
        tz, ty = (z - offset(slot) + NZ) % NZ, beside(y) if turn else y
        return remote(
            sources[a].at[:, columns(tz * 2 + half(ty))], landing(a, slot, y % 2),
            tile_send.at[a, turn, slot], tile_recv.at[a, turn, slot], device(tz, x, ty, c),
        )

    def tile_in(a, slot, turn):
        fz, fy = (z + offset(slot) + NZ) % NZ, beside(y) if turn else y
        return remote(
            sources[a].at[:, columns(fz * 2 + half(fy))], landing(a, slot, fy % 2),
            tile_send.at[a, turn, slot], tile_recv.at[a, turn, slot], device(fz, x, fy, c),
        )

    def tile_own(a):
        return pltpu.make_async_copy(
            sources[a].at[:, columns(z * 2 + half(y))], landing(a, 0, y % 2), own_sem.at[a]
        )

    for a in range(4):
        tile_own(a).start()
    for first in (0, 2):
        tile_out(first, 0, 1).start()
        tile_out(first + 1, 0, 1).start()

        def start(slot, carry):
            for turn in range(2):
                tile_out(first, slot, turn).start()
                tile_out(first + 1, slot, turn).start()
            return carry

        lax.fori_loop(1, NZ, start, 0)

    def chunk(a, part, dx, core, g):
        return kv.at[a, pl.ds(2 * part, 2), around(x, dx, NX), core, side if g == 0 else 1 - side]

    def along_x(a, part, g, leg):
        way = far_way(a, part)
        dx, to = {LONG1: (0, way), LONG2: (-way, way), SHORT: (0, -way)}[leg]
        ref = chunk(a, part, dx, c, g)
        return remote(
            ref, ref, x_send.at[a, part, g, leg], x_recv.at[a, part, g, leg],
            device(z, around(x, to, NX), y, c),
        )

    def from_x(a, part, g, leg):
        way = far_way(a, part)
        dx, of = {LONG1: (-way, -way), LONG2: (-2 * way, -way), SHORT: (way, way)}[leg]
        ref = chunk(a, part, dx, c, g)
        return dx, remote(
            ref, ref, x_send.at[a, part, g, leg], x_recv.at[a, part, g, leg],
            device(z, around(x, of, NX), y, c),
        )

    def over_y(a, part, dx, g):
        ref = chunk(a, part, dx, c, g)
        return remote(
            ref, ref, y_send.at[a, part, dx % NX], y_recv.at[a, part, dx % NX],
            device(z, x, NY - 1 - y, c),
        )

    def pair(a, part, dx, g, core):
        ref = chunk(a, part, dx, core, g)
        return remote(
            ref, ref, pair_send.at[a, part, g, dx % NX], pair_recv.at[a, part, g, dx % NX],
            device(z, x, y, 1 - c),
        )

    def entered(a, part):
        for slot in (2 * part, 2 * part + 1):
            for turn in range(2):
                if slot == 0 and turn == 0:
                    tile_own(a).wait()
                else:
                    tile_in(a, slot, turn).wait_recv()

    def got_x(a, part, g, leg):
        dx, copy = from_x(a, part, g, leg)
        copy.wait_recv()
        if leg == LONG1:
            along_x(a, part, g, LONG2).start()
        if a == 0:
            over_y(a, part, dx, 0).start()
        pair(a, part, dx, g, c).start()

    def stage_a(part):
        for a in (1, 0):
            entered(a, part)
            if a == 1:
                over_y(a, part, 0, 0).start()
            along_x(a, part, 0, LONG1).start()
            along_x(a, part, 0, SHORT).start()
            if a == 0:
                over_y(a, part, 0, 0).start()
            pair(a, part, 0, 0, c).start()

    def stage_b(part):
        over_y(1, part, 0, 1).wait_recv()
        along_x(1, part, 1, LONG1).start()
        along_x(1, part, 1, SHORT).start()
        pair(1, part, 0, 1, c).start()
        for a in (0, 1):
            got_x(a, part, 0, LONG1)
            got_x(a, part, 0, SHORT)

    def stage_c(part):
        got_x(1, part, 1, LONG1)
        got_x(1, part, 1, SHORT)
        got_x(0, part, 0, LONG2)
        got_x(1, part, 0, LONG2)

    def stage_d(part):
        got_x(1, part, 1, LONG2)
        for dx in range(NX):
            over_y(0, part, dx, 1).wait_recv()
            pair(0, part, dx, 1, c).start()

    stages = (stage_a, stage_b, stage_c, stage_d)
    for time in range(PARTS + len(stages) - 1):
        for late, stage in enumerate(stages):
            if 0 <= time - late < PARTS:
                stage(time - late)

    for a in (2, 3):
        tile_own(a).wait()
    for a in range(4):
        tile_out(a, 0, 1).wait_send()
        if a >= 2:
            tile_in(a, 0, 1).wait_recv()

    def finish(slot, carry):
        for turn in range(2):
            for a in range(4):
                tile_out(a, slot, turn).wait_send()
                if a >= 2:
                    tile_in(a, slot, turn).wait_recv()
        return carry

    lax.fori_loop(1, NZ, finish, 0)
    for part in range(PARTS):
        for a in range(2):
            for g in range(1 + a):
                for leg in range(3):
                    along_x(a, part, g, leg).wait_send()
            for dx in range(NX if a == 0 else 1):
                over_y(a, part, dx, 0).wait_send()
            for g in range(2):
                for dx in range(NX):
                    pair(a, part, dx, g, c).wait_send()
                    pair(a, part, dx, g, 1 - c).wait_recv()


def attend_kernel(
    lists, firsts, q, n, kv_hbm, att, dq, part, kv, acc, load_sem, store_sem,
):
    scaling = 1.0 / math.sqrt(DH)
    loads = [pltpu.make_async_copy(kv_hbm.at[a], kv.at[a], load_sem.at[a]) for a in range(2)]
    for load in loads:
        load.start()

    def clear(i, carry):
        for a in range(2):
            acc[a, pl.ds(i * 8, 8)] = jnp.zeros((8, BLK, DH), jnp.float32)
        return carry

    lax.fori_loop(0, NB // 8, clear, 0)
    for load in loads:
        load.wait()

    column = lax.broadcasted_iota(jnp.int32, (1, ENTRIES * BLK), 1) // BLK

    def dot(a, b, dims):
        return lax.dot_general(a, b, (dims, ((), ())), preferred_element_type=jnp.float32)

    def group(g, carry):
        ids = [g * GROUP + u for u in range(GROUP)]
        entries = [[lists[i, e] for e in range(ENTRIES)] for i in ids]
        qs = [q[i] for i in ids]
        ks = [jnp.concatenate([kv[0, e] for e in es], 0) for es in entries]
        scores = [dot(a, b, ((1,), (1,))) * scaling for a, b in zip(qs, ks)]
        masked = []
        for i, s in zip(ids, scores):
            block = firsts[i]
            gone = ((column == 0) & (block == 0)) | ((column == 2) & (block == NB - 1))
            masked.append(jnp.where(gone, -jnp.inf, s))
        raws = [jnp.exp(s - jnp.max(s, 1, keepdims=True)) for s in masked]
        probs = [r * (1.0 / jnp.sum(r, 1, keepdims=True)) for r in raws]
        probs_bf = [p.astype(jnp.bfloat16) for p in probs]
        vs = [jnp.concatenate([kv[1, e] for e in es], 0) for es in entries]
        atts = [dot(p, b, ((1,), (0,))).astype(jnp.bfloat16) for p, b in zip(probs_bf, vs)]
        grads = []
        for i, a in zip(ids, atts):
            att[i] = a
            grads.append((a.astype(jnp.float32) - n[i].astype(jnp.float32)).astype(jnp.bfloat16))
        dprobs = [dot(d, b, ((1,), (1,))) for d, b in zip(grads, vs)]
        dscores = [
            (p * (d - jnp.sum(p * d, 1, keepdims=True))).astype(jnp.bfloat16)
            for p, d in zip(probs, dprobs)
        ]
        for i, d, b in zip(ids, dscores, ks):
            dq[i] = (dot(d, b, ((1,), (0,))) * scaling).astype(jnp.bfloat16)
        dks = [dot(d, a, ((0,), (0,))) * scaling for d, a in zip(dscores, qs)]
        dvs = [dot(p, d, ((0,), (0,))) for p, d in zip(probs_bf, grads)]
        for es, dk, dv in zip(entries, dks, dvs):
            for e in range(ENTRIES):
                acc[0, es[e]] += dk[e * BLK : (e + 1) * BLK]
                acc[1, es[e]] += dv[e * BLK : (e + 1) * BLK]
        return carry

    lax.fori_loop(0, QUERIES // GROUP, group, 0)

    def store(a, i):
        span = pl.ds(i * 64, 64)
        return pltpu.make_async_copy(kv.at[a, span], part.at[a, span], store_sem.at[a, i])

    for a in range(2):
        def out(i, carry):
            def cast(s, inner):
                at = pl.ds(i * 64 + s * 8, 8)
                kv[a, at] = acc[a, at].astype(jnp.bfloat16)
                return inner

            lax.fori_loop(0, 8, cast, 0)
            store(a, i).start()
            return carry

        lax.fori_loop(0, NB // 64, out, 0)
    for a in range(2):
        def done(i, carry):
            store(a, i).wait()
            return carry

        lax.fori_loop(0, NB // 64, done, 0)


def return_kernel(
    att, dq, part_hbm, att_out, dq_out, dk_out, dv_out,
    own, sib, x_came, y_came, load_sem, pair_send, pair_recv, x_send, x_recv, y_send, y_recv,
    tile_send, tile_recv, tile_sem,
):
    z, x, y, c = place()
    greet(z, x, y, c)
    side = y // 2

    def load(a, part):
        return pltpu.make_async_copy(
            part_hbm.at[a, pl.ds(2 * part, 2), :, c], own.at[a, part], load_sem.at[a, part]
        )

    def pair(a, part):
        return remote(
            part_hbm.at[a, pl.ds(2 * part, 2), :, 1 - c], sib.at[a, part],
            pair_send.at[a, part], pair_recv.at[a, part], device(z, x, y, 1 - c),
        )

    order = tuple(reversed(range(PARTS)))
    for part in order:
        for a in (0, 1):
            pair(a, part).start()
            load(a, part).start()

    outs = (dk_out, dv_out, att_out, dq_out)

    def source(a, slot, row):
        if a < 2:
            return own.at[a, slot // 2, slot % 2, x, side, rows(row)]
        return (att, dq)[a - 2].at[slot, rows(row)]

    def tile_out(a, slot, turn):
        tz, ty = (z + offset(slot) + NZ) % NZ, beside(y) if turn else y
        return remote(
            source(a, slot, ty % 2), outs[a].at[:, columns(z * 2 + half(y))],
            tile_send.at[a, turn, slot], tile_recv.at[a, turn, slot], device(tz, x, ty, c),
        )

    def tile_in(a, slot, turn):
        fz, fy = (z - offset(slot) + NZ) % NZ, beside(y) if turn else y
        return remote(
            source(a, slot, y % 2), outs[a].at[:, columns(fz * 2 + half(fy))],
            tile_send.at[a, turn, slot], tile_recv.at[a, turn, slot], device(fz, x, fy, c),
        )

    def tile_own(a):
        return pltpu.make_async_copy(
            source(a, 0, y % 2), outs[a].at[:, columns(z * 2 + half(y))], tile_sem.at[a]
        )

    for a in (2, 3):
        tile_own(a).start()
        tile_out(a, 0, 1).start()

    def start(slot, carry):
        for turn in range(2):
            tile_out(2, slot, turn).start()
            tile_out(3, slot, turn).start()
        return carry

    lax.fori_loop(1, NZ, start, 0)

    def sum_up(a, part, dx, g, first, came):
        xs, gs = around(x, dx, NX), side if g == 0 else 1 - side

        def span(i, carry):
            at = rows(i % 2)
            total = own[a, part, i // 2, xs, gs, at].astype(jnp.float32)
            if first:
                total += sib[a, part, i // 2, xs, gs, at].astype(jnp.float32)
            for ref in came:
                total += ref[i // 2, at].astype(jnp.float32)
            own[a, part, i // 2, xs, gs, at] = total.astype(jnp.bfloat16)
            return carry

        lax.fori_loop(0, 4, span, 0)

    def chunk(a, part, dx, g):
        return own.at[a, part, :, around(x, dx, NX), side if g == 0 else 1 - side]

    def landed_x(a, part, g, leg):
        return x_came.at[a + g, part, leg]

    def landed_y(a, part, dx):
        return y_came.at[part, dx % NX if a == 0 else NX]

    def along_x(a, part, g, leg):
        way = far_way(a, part)
        dx, to = {LONG1: (2 * way, way), LONG2: (way, way), SHORT: (-way, -way)}[leg]
        return remote(
            chunk(a, part, dx, g), landed_x(a, part, g, leg), x_send.at[a, part, g, leg],
            x_recv.at[a, part, g, leg], device(z, around(x, to, NX), y, c),
        )

    def over_y(a, part, dx):
        return remote(
            chunk(a, part, dx, 1), landed_y(a, part, dx), y_send.at[a, part, dx % NX],
            y_recv.at[a, part, dx % NX], device(z, x, NY - 1 - y, c),
        )

    def send_tiles(a, part):
        for slot in (2 * part, 2 * part + 1):
            for turn in range(2):
                if slot == 0 and turn == 0:
                    tile_own(a).start()
                else:
                    tile_out(a, slot, turn).start()

    def first_legs(a, part, g, first):
        way = far_way(a, part)
        for dx, leg in ((2 * way, LONG1), (-way, SHORT)):
            sum_up(a, part, dx, g, first, [] if a else [landed_y(a, part, dx)])
            along_x(a, part, g, leg).start()

    def second_leg(a, part, g, first):
        along_x(a, part, g, LONG1).wait_recv()
        dx = far_way(a, part)
        came = [landed_x(a, part, g, LONG1)] + ([] if a else [landed_y(a, part, dx)])
        sum_up(a, part, dx, g, first, came)
        along_x(a, part, g, LONG2).start()

    def last_sum(a, part, g, first):
        along_x(a, part, g, LONG2).wait_recv()
        along_x(a, part, g, SHORT).wait_recv()
        came = [landed_x(a, part, g, LONG2), landed_x(a, part, g, SHORT)]
        sum_up(a, part, 0, g, first, came + ([] if a else [landed_y(a, part, 0)]))

    def stage_a(part):
        for a in (0, 1):
            load(a, part).wait()
            pair(a, part).wait_recv()
            if a == 0:
                way = far_way(a, part)
                for dx in (2 * way, -way, way, 0):
                    sum_up(a, part, dx, 1, True, [])
                    over_y(a, part, dx).start()
            else:
                for g in (1, 0):
                    first_legs(a, part, g, True)

    def stage_b(part):
        for dx in range(NX):
            over_y(0, part, dx).wait_recv()
        first_legs(0, part, 0, True)
        second_leg(1, part, 1, True)
        second_leg(1, part, 0, True)

    def stage_c(part):
        second_leg(0, part, 0, True)
        last_sum(1, part, 1, True)
        over_y(1, part, 0).start()

    def stage_d(part):
        last_sum(0, part, 0, True)
        send_tiles(0, part)
        last_sum(1, part, 0, True)
        over_y(1, part, 0).wait_recv()
        sum_up(1, part, 0, 0, False, [landed_y(1, part, 0)])
        send_tiles(1, part)

    stages = (stage_a, stage_b, stage_c, stage_d)
    for time in range(PARTS + len(stages) - 1):
        for late, stage in enumerate(stages):
            if 0 <= time - late < PARTS:
                stage(order[time - late])

    for a in range(4):
        tile_own(a).wait()
        tile_out(a, 0, 1).wait_send()
        tile_in(a, 0, 1).wait_recv()

    def finish(slot, carry):
        for turn in range(2):
            for a in range(4):
                tile_out(a, slot, turn).wait_send()
                tile_in(a, slot, turn).wait_recv()
        return carry

    lax.fori_loop(1, NZ, finish, 0)
    for part in range(PARTS):
        for a in range(2):
            pair(a, part).wait_send()
            for g in range(1 + a):
                for leg in range(3):
                    along_x(a, part, g, leg).wait_send()
            for dx in range(NX if a == 0 else 1):
                over_y(a, part, dx).wait_send()


ANY = pl.BlockSpec(memory_space=pl.ANY)
VMEM = pl.BlockSpec(memory_space=pltpu.VMEM)
SMEM = pl.BlockSpec(memory_space=pltpu.SMEM)
DMA = pltpu.SemaphoreType.DMA


def bf16(*shape):
    return jax.ShapeDtypeStruct(shape, jnp.bfloat16)


def copies(*shape):
    return [DMA(shape), DMA(shape)]


def shards(queries, keys, values, noise, random_blocks, global_blocks):
    z, x, y, c = place()
    gathered = (2, NZ, NX, NC, 2, SIDE, DH)
    q_all, n_all, kv = pl.pallas_call(
        fetch_kernel,
        name="fetch",
        out_shape=(bf16(NZ, SIDE, DH), bf16(NZ, SIDE, DH), bf16(*gathered)),
        in_specs=[ANY] * 4,
        out_specs=(ANY,) * 3,
        scratch_shapes=[
            *copies(4, 2, NZ), DMA((4,)), *copies(2, PARTS, 2, 3), *copies(2, PARTS, NX),
            *copies(2, PARTS, 2, NX),
        ],
        compiler_params=pltpu.CompilerParams(collective_id=0, has_side_effects=True),
    )(queries, keys, values, noise)

    at = jnp.arange(QUERIES, dtype=jnp.int32)
    planes = (z + offset(at // 4) + NZ) % NZ
    firsts = ((planes * NX + x) * NC + c) * PER + y // 2 * 4 + at % 4
    window = jnp.clip(firsts[:, None] + jnp.arange(-1, 2, dtype=jnp.int32)[None], 0, NB - 1)
    lists = jnp.concatenate(
        [window, random_blocks[firsts], jnp.broadcast_to(global_blocks[None], (QUERIES, 2))], 1
    ).astype(jnp.int32)
    away = (lists // 64 - z + NZ) % NZ
    slots = jnp.where(away <= 4, jnp.maximum(2 * away - 1, 0), 2 * (NZ - away))
    lists = slots * 64 + lists % 64

    att, dq, part = pl.pallas_call(
        attend_kernel,
        name="attend",
        out_shape=(bf16(QUERIES, BLK, DH), bf16(QUERIES, BLK, DH), bf16(2, NB, BLK, DH)),
        in_specs=[SMEM, SMEM, VMEM, VMEM, ANY],
        out_specs=(VMEM, VMEM, ANY),
        scratch_shapes=[
            pltpu.VMEM((2, NB, BLK, DH), jnp.bfloat16),
            pltpu.VMEM((2, NB, BLK, DH), jnp.float32),
            DMA((2,)), DMA((2, NB // 64)),
        ],
        compiler_params=pltpu.CompilerParams(vmem_limit_bytes=60 * 2**20),
    )(
        lists, firsts, q_all.reshape(QUERIES, BLK, DH), n_all.reshape(QUERIES, BLK, DH),
        kv.reshape(2, NB, BLK, DH),
    )

    outs = pl.pallas_call(
        return_kernel,
        name="give_back",
        out_shape=(bf16(ROWS, HEADS * DH),) * 4,
        in_specs=[ANY] * 3,
        out_specs=(ANY,) * 4,
        scratch_shapes=[
            pltpu.VMEM((2, PARTS, 2, NX, 2, SIDE, DH), jnp.bfloat16),
            pltpu.VMEM((2, PARTS, 2, NX, 2, SIDE, DH), jnp.bfloat16),
            pltpu.VMEM((3, PARTS, 3, 2, SIDE, DH), jnp.bfloat16),
            pltpu.VMEM((PARTS, NX + 1, 2, SIDE, DH), jnp.bfloat16),
            DMA((2, PARTS)), *copies(2, PARTS), *copies(2, PARTS, 2, 3), *copies(2, PARTS, NX),
            *copies(4, 2, NZ), DMA((4,)),
        ],
        compiler_params=pltpu.CompilerParams(
            collective_id=1, has_side_effects=True, vmem_limit_bytes=40 * 2**20
        ),
    )(att.reshape(NZ, SIDE, DH), dq.reshape(NZ, SIDE, DH), part.reshape(gathered))
    return tuple(outs)


def solution(mesh):
    rows = P(("seq", "head"), None)
    return jax.shard_map(
        shards,
        mesh=mesh,
        in_specs=(rows, rows, rows, rows, P(), P()),
        out_specs=(rows, rows, rows, rows),
        check_vma=False,
    )
```

```python
import math

import jax
import jax.numpy as jnp
from jax import lax
from jax.experimental import pallas as pl
from jax.experimental.pallas import tpu as pltpu
from jax.sharding import PartitionSpec as P

DH = 128
BLK = 64
NX, NY, NZ, NC = 4, 4, 8, 2
ROWS = 128
SIDE = 2 * ROWS
SHARD = NY * ROWS
PER = SHARD // BLK
NB = NZ * NX * NC * PER
QUERIES = NZ * SIDE // BLK
HEADS = 16
ENTRIES = 8
GROUP = 8
FETCH_MIB, ATTEND_MIB, RETURN_MIB = 4, 8, 26
MESH = pl.DeviceIdType.MESH


def place():
    seq, y = lax.axis_index("seq"), lax.axis_index("head")
    return seq // (NX * NC), (seq // NC) % NX, y, seq % NC


def device(z, x, y, c):
    return ((z * NX + x) * NC + c, y)


def around(base, step, count):
    return (base + step + count) % count


def offset(slot):
    return (slot + 1) // 2 * (2 * (slot % 2) - 1)


def beside(y):
    return y + 1 - 2 * (y % 2)


def half(y):
    return (y + 1) // 2 % 2


def greet(z, x, y, c):
    barrier = pltpu.get_barrier_semaphore()

    def signal(target):
        pl.semaphore_signal(barrier, inc=1, device_id=target, device_id_type=MESH)

    def plane(dz, carry):
        signal(device((z + dz) % NZ, x, y, c))
        signal(device((z + dz) % NZ, x, beside(y), c))
        return carry

    lax.fori_loop(1, NZ, plane, 0)
    signal(device(z, x, beside(y), c))
    signal(device(z, around(x, 1, NX), y, c))
    signal(device(z, around(x, -1, NX), y, c))
    signal(device(z, x, NY - 1 - y, c))
    signal(device(z, x, y, 1 - c))
    pl.semaphore_wait(barrier, 2 * NZ - 1 + 4)


def remote(src, dst, send, recv, target):
    return pltpu.make_async_remote_copy(
        src_ref=src, dst_ref=dst, send_sem=send, recv_sem=recv, device_id=target, device_id_type=MESH
    )


def columns(h):
    return pl.ds(pl.multiple_of(h * DH, DH), DH)


def rows(at):
    return pl.ds(pl.multiple_of(at * ROWS, ROWS), ROWS)


def far_way(a, part):
    return 1 if (a + part) % 2 == 0 else -1


def x_first(a, part):
    return a == 0 and part != 4


def sides(a, part):
    return (0,) if x_first(a, part) else (1, 0)


def over_count(a, part):
    return NX if x_first(a, part) else 1


LONG1, LONG2, SHORT = 0, 1, 2


def fetch_kernel(
    q, k, v, n, q_out, n_out, kv, cleared,
    tile_send, tile_recv, own_sem, x_send, x_recv, y_send, y_recv, pair_send, pair_recv,
    zeros, clear_sem,
):
    z, x, y, c = place()
    greet(z, x, y, c)
    side = y // 2
    sources = (k, v, q, n)

    def landing(a, slot, row):
        if a < 2:
            return kv.at[a, slot, x, c, side, rows(row)]
        return (q_out, n_out)[a - 2].at[slot, rows(row)]

    def tile_out(a, slot, turn):
        tz, ty = (z - offset(slot) + NZ) % NZ, beside(y) if turn else y
        return remote(
            sources[a].at[:, columns(tz * 2 + half(ty))], landing(a, slot, y % 2),
            tile_send.at[a, turn, slot], tile_recv.at[a, turn, slot], device(tz, x, ty, c),
        )

    def tile_in(a, slot, turn):
        fz, fy = (z + offset(slot) + NZ) % NZ, beside(y) if turn else y
        return remote(
            sources[a].at[:, columns(fz * 2 + half(fy))], landing(a, slot, fy % 2),
            tile_send.at[a, turn, slot], tile_recv.at[a, turn, slot], device(fz, x, fy, c),
        )

    def tile_own(a):
        return pltpu.make_async_copy(
            sources[a].at[:, columns(z * 2 + half(y))], landing(a, 0, y % 2), own_sem.at[a]
        )

    for a in range(4):
        tile_own(a).start()

    def send_tiles(first):
        tile_out(first, 0, 1).start()
        tile_out(first + 1, 0, 1).start()

        def start(slot, carry):
            for turn in range(2):
                tile_out(first, slot, turn).start()
                tile_out(first + 1, slot, turn).start()
            return carry

        lax.fori_loop(1, NZ, start, 0)

    send_tiles(0)

    def chunk(a, part, dx, core, g):
        return kv.at[a, part, around(x, dx, NX), core, side if g == 0 else 1 - side]

    def along_x(a, part, g, leg):
        way = far_way(a, part)
        dx, to = {LONG1: (0, way), LONG2: (-way, way), SHORT: (0, -way)}[leg]
        ref = chunk(a, part, dx, c, g)
        return remote(
            ref, ref, x_send.at[a, part, g, leg], x_recv.at[a, part, g, leg],
            device(z, around(x, to, NX), y, c),
        )

    def from_x(a, part, g, leg):
        way = far_way(a, part)
        dx, of = {LONG1: (-way, -way), LONG2: (-2 * way, -way), SHORT: (way, way)}[leg]
        ref = chunk(a, part, dx, c, g)
        return dx, remote(
            ref, ref, x_send.at[a, part, g, leg], x_recv.at[a, part, g, leg],
            device(z, around(x, of, NX), y, c),
        )

    def over_y(a, part, dx, g):
        ref = chunk(a, part, dx, c, g)
        return remote(
            ref, ref, y_send.at[a, part, dx % NX], y_recv.at[a, part, dx % NX],
            device(z, x, NY - 1 - y, c),
        )

    def pair(a, part, dx, g, core):
        ref = chunk(a, part, dx, core, g)
        return remote(
            ref, ref, pair_send.at[a, part, g, dx % NX], pair_recv.at[a, part, g, dx % NX],
            device(z, x, y, 1 - c),
        )

    def entered(a, part):
        for turn in range(2):
            if part == 0 and turn == 0:
                tile_own(a).wait()
            else:
                tile_in(a, part, turn).wait_recv()

    def got_x(a, part, g, leg):
        dx, copy = from_x(a, part, g, leg)
        copy.wait_recv()
        if leg == LONG1:
            along_x(a, part, g, LONG2).start()
        if x_first(a, part):
            over_y(a, part, dx, 0).start()
        pair(a, part, dx, g, c).start()

    def stage_a(part):
        for a in (1, 0):
            entered(a, part)
            over_y(a, part, 0, 0).start()
            along_x(a, part, 0, LONG1).start()
            along_x(a, part, 0, SHORT).start()
            pair(a, part, 0, 0, c).start()

    def stage_b(part):
        for a in (1, 0):
            if not x_first(a, part):
                over_y(a, part, 0, 1).wait_recv()
                along_x(a, part, 1, LONG1).start()
                along_x(a, part, 1, SHORT).start()
                pair(a, part, 0, 1, c).start()
        for a in (0, 1):
            got_x(a, part, 0, LONG1)
            got_x(a, part, 0, SHORT)

    def stage_c(part):
        for a in (1, 0):
            if not x_first(a, part):
                got_x(a, part, 1, LONG1)
                got_x(a, part, 1, SHORT)
        got_x(0, part, 0, LONG2)
        got_x(1, part, 0, LONG2)

    def stage_d(part):
        for a in (1, 0):
            if x_first(a, part):
                for dx in range(NX):
                    over_y(a, part, dx, 1).wait_recv()
                    pair(a, part, dx, 1, c).start()
            else:
                got_x(a, part, 1, LONG2)

    def clear(a, i):
        return pltpu.make_async_copy(zeros, cleared.at[a, pl.ds(i * 64, 64)], clear_sem.at[a, i])

    stages = (stage_a, stage_b, stage_c, stage_d)
    for time in range(NZ + len(stages) - 1):
        for late, stage in enumerate(stages):
            if 0 <= time - late < NZ:
                stage(time - late)
        if time == 0:
            zeros[...] = jnp.zeros(zeros.shape, jnp.bfloat16)
            for a in range(2):
                for i in range(NB // 64):
                    clear(a, i).start()
        if time == 4:
            send_tiles(2)

    for a in range(2):
        for i in range(NB // 64):
            clear(a, i).wait()
    for a in (2, 3):
        tile_own(a).wait()
    for a in range(4):
        tile_out(a, 0, 1).wait_send()
        if a >= 2:
            tile_in(a, 0, 1).wait_recv()

    def finish(slot, carry):
        for turn in range(2):
            for a in range(4):
                tile_out(a, slot, turn).wait_send()
                if a >= 2:
                    tile_in(a, slot, turn).wait_recv()
        return carry

    lax.fori_loop(1, NZ, finish, 0)
    for part in range(NZ):
        for a in range(2):
            for g in sides(a, part):
                for leg in range(3):
                    along_x(a, part, g, leg).wait_send()
            for dx in range(over_count(a, part)):
                over_y(a, part, dx, 0).wait_send()
            for g in range(2):
                for dx in range(NX):
                    pair(a, part, dx, g, c).wait_send()
                    pair(a, part, dx, g, 1 - c).wait_recv()


def attend_kernel(random_blocks, global_blocks, q, n, kv, cleared, att, dq, acc, global_sum):
    scaling = 1.0 / math.sqrt(DH)
    z, x, y, c = place()
    side = y // 2
    global_sum[...] = jnp.zeros(global_sum.shape, jnp.float32)
    column = lax.broadcasted_iota(jnp.int32, (1, ENTRIES * BLK), 1) // BLK

    def lies(block):
        away = ((block >> 6) - z) & (NZ - 1)
        slot = jnp.where(away <= NZ // 2, jnp.maximum(2 * away - 1, 0), 2 * (NZ - away))
        return slot * 64 + (block & 63)

    def dot(a, b, dims):
        return lax.dot_general(a, b, (dims, ((), ())), preferred_element_type=jnp.float32)

    globals_at = [lies(global_blocks[e]) for e in range(2)]

    def add(a, at, term):
        acc[a, at] = (acc[a, at].astype(jnp.float32) + term).astype(jnp.bfloat16)

    def group(g, carry):
        ids = [g * GROUP + u for u in range(GROUP)]
        blocks, entries = [], []
        for u in range(GROUP):
            plane = (z + offset(g * (GROUP // 4) + u // 4)) & (NZ - 1)
            block = ((plane * NX + x) * NC + c) * PER + side * 4 + u % 4
            blocks.append(block)
            near = [jnp.maximum(block - 1, 0), block, jnp.minimum(block + 1, NB - 1)]
            near += [random_blocks[e, block] for e in range(3)]
            entries.append([lies(b) for b in near] + globals_at)
        qs = [q[i] for i in ids]
        ks = [jnp.concatenate([kv[0, e] for e in es], 0) for es in entries]
        scores = [dot(a, b, ((1,), (1,))) * scaling for a, b in zip(qs, ks)]
        masked = []
        for u, (block, s) in enumerate(zip(blocks, scores)):
            if u % 4 == 0:
                s = jnp.where((column == 0) & (block == 0), -jnp.inf, s)
            if u % 4 == 3:
                s = jnp.where((column == 2) & (block == NB - 1), -jnp.inf, s)
            masked.append(s)
        raws = [jnp.exp(s - jnp.max(s, 1, keepdims=True)) for s in masked]
        probs = [r * (1.0 / jnp.sum(r, 1, keepdims=True)) for r in raws]
        probs_bf = [p.astype(jnp.bfloat16) for p in probs]
        vs = [jnp.concatenate([kv[1, e] for e in es], 0) for es in entries]
        atts = [dot(p, b, ((1,), (0,))).astype(jnp.bfloat16) for p, b in zip(probs_bf, vs)]
        grads = []
        for i, a in zip(ids, atts):
            att[i] = a
            grads.append((a.astype(jnp.float32) - n[i].astype(jnp.float32)).astype(jnp.bfloat16))
        dprobs = [dot(d, b, ((1,), (1,))) for d, b in zip(grads, vs)]
        dscores = [
            (p * (d - jnp.sum(p * d, 1, keepdims=True))).astype(jnp.bfloat16)
            for p, d in zip(probs, dprobs)
        ]
        for i, d, b in zip(ids, dscores, ks):
            dq[i] = (dot(d, b, ((1,), (0,))) * scaling).astype(jnp.bfloat16)
        terms = (
            [dot(d, a, ((0,), (0,))) * scaling for d, a in zip(dscores, qs)],
            [dot(p, d, ((0,), (0,))) for p, d in zip(probs_bf, grads)],
        )

        for a in range(2):
            def term(u, e):
                return terms[a][u][e * BLK : (e + 1) * BLK]

            for first in range(0, GROUP, 4):
                last = first + 3
                add(a, entries[first][0], term(first, 0))
                for u in range(first, last + 1):
                    total = term(u, 1)
                    if u > first:
                        total += term(u - 1, 2)
                    if u < last:
                        total += term(u + 1, 0)
                    add(a, entries[u][1], total)
                add(a, entries[last][2], term(last, 2))
            for u in range(GROUP):
                for e in range(3, 6):
                    add(a, entries[u][e], term(u, e))
            for e in range(2):
                global_sum[a, e] += sum(term(u, 6 + e) for u in range(GROUP))
        return carry

    lax.fori_loop(0, QUERIES // GROUP, group, 0)
    for a in range(2):
        for e in range(2):
            add(a, globals_at[e], global_sum[a, e])


def return_kernel(
    att, dq, partial, att_out, dq_out, dk_out, dv_out,
    own, sib, x_came, y_came, pair_send, pair_recv, x_send, x_recv, y_send, y_recv,
    tile_send, tile_recv, tile_sem,
):
    z, x, y, c = place()
    greet(z, x, y, c)
    side = y // 2

    def pair(a, part):
        return remote(
            partial.at[a, part, :, 1 - c], sib.at[a, part],
            pair_send.at[a, part], pair_recv.at[a, part], device(z, x, y, 1 - c),
        )

    order = tuple(reversed(range(NZ)))
    for part in order:
        for a in (0, 1):
            pair(a, part).start()

    outs = (dk_out, dv_out, att_out, dq_out)

    def source(a, slot, row):
        if a < 2:
            return own.at[a, slot, x, side, rows(row)]
        return (att, dq)[a - 2].at[slot, rows(row)]

    def tile_out(a, slot, turn):
        tz, ty = (z + offset(slot) + NZ) % NZ, beside(y) if turn else y
        return remote(
            source(a, slot, ty % 2), outs[a].at[:, columns(z * 2 + half(y))],
            tile_send.at[a, turn, slot], tile_recv.at[a, turn, slot], device(tz, x, ty, c),
        )

    def tile_in(a, slot, turn):
        fz, fy = (z - offset(slot) + NZ) % NZ, beside(y) if turn else y
        return remote(
            source(a, slot, y % 2), outs[a].at[:, columns(fz * 2 + half(fy))],
            tile_send.at[a, turn, slot], tile_recv.at[a, turn, slot], device(fz, x, fy, c),
        )

    def tile_own(a):
        return pltpu.make_async_copy(
            source(a, 0, y % 2), outs[a].at[:, columns(z * 2 + half(y))], tile_sem.at[a]
        )

    for a in (2, 3):
        tile_own(a).start()
        tile_out(a, 0, 1).start()

    def start(slot, carry):
        for turn in range(2):
            tile_out(2, slot, turn).start()
            tile_out(3, slot, turn).start()
        return carry

    lax.fori_loop(1, NZ, start, 0)

    def sum_up(a, part, dx, g, first, came):
        xs, gs = around(x, dx, NX), side if g == 0 else 1 - side

        def span(i, carry):
            at = rows(i)
            if first:
                total = partial[a, part, xs, c, gs, at].astype(jnp.float32)
                total += sib[a, part, xs, gs, at].astype(jnp.float32)
            else:
                total = own[a, part, xs, gs, at].astype(jnp.float32)
            for ref in came:
                total += ref[at].astype(jnp.float32)
            own[a, part, xs, gs, at] = total.astype(jnp.bfloat16)
            return carry

        lax.fori_loop(0, 2, span, 0)

    def chunk(a, part, dx, g):
        return own.at[a, part, around(x, dx, NX), side if g == 0 else 1 - side]

    def landed_x(a, part, g, leg):
        return x_came.at[2 * a + g, part, leg]

    def landed_y(a, part, dx):
        return y_came.at[part, dx % NX if a == 0 else NX]

    def along_x(a, part, g, leg):
        way = far_way(a, part)
        dx, to = {LONG1: (2 * way, way), LONG2: (way, way), SHORT: (-way, -way)}[leg]
        return remote(
            chunk(a, part, dx, g), landed_x(a, part, g, leg), x_send.at[a, part, g, leg],
            x_recv.at[a, part, g, leg], device(z, around(x, to, NX), y, c),
        )

    def over_y(a, part, dx):
        return remote(
            chunk(a, part, dx, 1), landed_y(a, part, dx), y_send.at[a, part, dx % NX],
            y_recv.at[a, part, dx % NX], device(z, x, NY - 1 - y, c),
        )

    def send_tiles(a, part):
        for turn in range(2):
            if part == 0 and turn == 0:
                tile_own(a).start()
            else:
                tile_out(a, part, turn).start()

    def leg(a, part, g, dx, name, came):
        if x_first(a, part):
            over_y(a, part, dx).wait_recv()
            came = came + [landed_y(a, part, dx)]
        sum_up(a, part, dx, g, True, came)
        along_x(a, part, g, name).start()

    def first_legs(a, part):
        way = far_way(a, part)
        for g in sides(a, part):
            leg(a, part, g, 2 * way, LONG1, [])
            leg(a, part, g, -way, SHORT, [])

    def last_sum(a, part, g):
        along_x(a, part, g, LONG2).wait_recv()
        along_x(a, part, g, SHORT).wait_recv()
        came = [landed_x(a, part, g, LONG2), landed_x(a, part, g, SHORT)]
        if x_first(a, part):
            over_y(a, part, 0).wait_recv()
            came = came + [landed_y(a, part, 0)]
        sum_up(a, part, 0, g, True, came)

    def begin(part):
        for a in range(2):
            pair(a, part).wait_recv()
            if x_first(a, part):
                way = far_way(a, part)
                for dx in (2 * way, -way, way, 0):
                    sum_up(a, part, dx, 1, True, [])
                    over_y(a, part, dx).start()
            else:
                first_legs(a, part)

    def after_y(part):
        for a in range(2):
            if x_first(a, part):
                first_legs(a, part)

    def seconds(part):
        for a in (1, 0):
            for g in sides(a, part):
                along_x(a, part, g, LONG1).wait_recv()
                leg(a, part, g, far_way(a, part), LONG2, [landed_x(a, part, g, LONG1)])

    def over(part):
        for a in (1, 0):
            if not x_first(a, part):
                last_sum(a, part, 1)
                over_y(a, part, 0).start()

    def lasts(part):
        for a in range(2):
            last_sum(a, part, 0)
            if not x_first(a, part):
                over_y(a, part, 0).wait_recv()
                sum_up(a, part, 0, 0, False, [landed_y(a, part, 0)])
            send_tiles(a, part)

    plan = ((after_y, 1), (begin, 0), (seconds, 2), (over, 3), (lasts, 4))
    for time in range(NZ + 4):
        for stage, late in plan:
            if 0 <= time - late < NZ:
                stage(order[time - late])

    for a in range(4):
        tile_own(a).wait()
        tile_out(a, 0, 1).wait_send()
        tile_in(a, 0, 1).wait_recv()

    def finish(slot, carry):
        for turn in range(2):
            for a in range(4):
                tile_out(a, slot, turn).wait_send()
                tile_in(a, slot, turn).wait_recv()
        return carry

    lax.fori_loop(1, NZ, finish, 0)
    for part in range(NZ):
        for a in range(2):
            pair(a, part).wait_send()
            for g in sides(a, part):
                for name in range(3):
                    along_x(a, part, g, name).wait_send()
            for dx in range(over_count(a, part)):
                over_y(a, part, dx).wait_send()


def write_kernel(*refs):
    moves = [pltpu.make_async_copy(refs[i], refs[4 + i], refs[8].at[i]) for i in range(4)]
    for move in moves:
        move.start()
    for move in moves:
        move.wait()


ANY = pl.BlockSpec(memory_space=pl.ANY)
VMEM = pl.BlockSpec(memory_space=pltpu.VMEM)
SMEM = pl.BlockSpec(memory_space=pltpu.SMEM)
DMA = pltpu.SemaphoreType.DMA


def bf16(*shape):
    return jax.ShapeDtypeStruct(shape, jnp.bfloat16)


def copies(*shape):
    return [DMA(shape), DMA(shape)]


def shards(queries, keys, values, noise, random_blocks, global_blocks):
    gathered = (2, NZ, NX, NC, 2, SIDE, DH)
    q_all, n_all, kv, cleared = pl.pallas_call(
        fetch_kernel,
        name="fetch",
        out_shape=(
            bf16(NZ, SIDE, DH), bf16(NZ, SIDE, DH), bf16(*gathered), bf16(2, NB, BLK, DH)
        ),
        in_specs=[ANY] * 4,
        out_specs=(ANY, ANY, ANY, ANY),
        scratch_shapes=[
            *copies(4, 2, NZ), DMA((4,)), *copies(2, NZ, 2, 3), *copies(2, NZ, NX),
            *copies(2, NZ, 2, NX), pltpu.VMEM((64, BLK, DH), jnp.bfloat16), DMA((2, NB // 64)),
        ],
        compiler_params=pltpu.CompilerParams(
            collective_id=0, has_side_effects=True, vmem_limit_bytes=FETCH_MIB * 2**20
        ),
    )(queries, keys, values, noise)

    att, dq, partial = pl.pallas_call(
        attend_kernel,
        name="attend",
        out_shape=(bf16(QUERIES, BLK, DH), bf16(QUERIES, BLK, DH), bf16(2, NB, BLK, DH)),
        in_specs=[SMEM, SMEM, VMEM, VMEM, VMEM, VMEM],
        out_specs=(VMEM, VMEM, VMEM),
        scratch_shapes=[pltpu.VMEM((2, 2, BLK, DH), jnp.float32)],
        input_output_aliases={5: 2},
        compiler_params=pltpu.CompilerParams(vmem_limit_bytes=ATTEND_MIB * 2**20),
    )(
        random_blocks.T, global_blocks, q_all.reshape(QUERIES, BLK, DH),
        n_all.reshape(QUERIES, BLK, DH), kv.reshape(2, NB, BLK, DH), cleared,
    )

    outs = pl.pallas_call(
        return_kernel,
        name="give_back",
        out_shape=(bf16(ROWS, HEADS * DH),) * 4,
        in_specs=[ANY, ANY, VMEM],
        out_specs=(ANY,) * 4,
        scratch_shapes=[
            pltpu.VMEM((2, NZ, NX, 2, SIDE, DH), jnp.bfloat16),
            pltpu.VMEM((2, NZ, NX, 2, SIDE, DH), jnp.bfloat16),
            pltpu.VMEM((4, NZ, 3, SIDE, DH), jnp.bfloat16),
            pltpu.VMEM((NZ, NX + 1, SIDE, DH), jnp.bfloat16),
            *copies(2, NZ), *copies(2, NZ, 2, 3), *copies(2, NZ, NX),
            *copies(4, 2, NZ), DMA((4,)),
        ],
        compiler_params=pltpu.CompilerParams(
            collective_id=1, has_side_effects=True, vmem_limit_bytes=RETURN_MIB * 2**20
        ),
    )(att.reshape(NZ, SIDE, DH), dq.reshape(NZ, SIDE, DH), partial.reshape(gathered))
    return pl.pallas_call(
        write_kernel,
        name="write",
        out_shape=(bf16(ROWS, HEADS * DH),) * 4,
        in_specs=[VMEM] * 4,
        out_specs=(ANY,) * 4,
        scratch_shapes=[DMA((4,))],
        compiler_params=pltpu.CompilerParams(vmem_limit_bytes=2**20),
    )(*outs)


def solution(mesh):
    rows = P(("seq", "head"), None)
    return jax.shard_map(
        shards,
        mesh=mesh,
        in_specs=(rows, rows, rows, rows, P(), P()),
        out_specs=(rows, rows, rows, rows),
        check_vma=False,
    )
```

```python
import math

import jax
import jax.numpy as jnp
from jax import lax
from jax.experimental import pallas as pl
from jax.experimental.pallas import tpu as pltpu
from jax.sharding import PartitionSpec as P

DH = 128
BLK = 64
NX, NY, NZ, NC = 4, 4, 8, 2
ROWS = 128
SIDE = 2 * ROWS
SHARD = NY * ROWS
PER = SHARD // BLK
NB = NZ * NX * NC * PER
QUERIES = NZ * SIDE // BLK
HEADS = 16
ENTRIES = 8
GROUP = 8
FETCH_MIB, ATTEND_MIB, RETURN_MIB = 4, 8, 26
MESH = pl.DeviceIdType.MESH


def place():
    seq, y = lax.axis_index("seq"), lax.axis_index("head")
    return lax.div(seq, NX * NC), lax.rem(lax.div(seq, NC), NX), y, lax.rem(seq, NC)


def device(z, x, y, c):
    return ((z * NX + x) * NC + c, y)


def around(base, step, count):
    return lax.rem(base + step % count, count)


def offset(slot):
    return (slot + 1) // 2 * (2 * (slot % 2) - 1)


def beside(y):
    return y + 1 - 2 * lax.rem(y, 2)


def half(y):
    return lax.rem(lax.div(y + 1, 2), 2)


def greet(z, x, y, c):
    barrier = pltpu.get_barrier_semaphore()

    def signal(target):
        pl.semaphore_signal(barrier, inc=1, device_id=target, device_id_type=MESH)

    for dz in range(1, NZ):
        signal(device(around(z, dz, NZ), x, y, c))
        signal(device(around(z, dz, NZ), x, beside(y), c))
    signal(device(z, x, beside(y), c))
    signal(device(z, around(x, 1, NX), y, c))
    signal(device(z, around(x, -1, NX), y, c))
    signal(device(z, x, NY - 1 - y, c))
    signal(device(z, x, y, 1 - c))
    pl.semaphore_wait(barrier, 2 * NZ - 1 + 4)


def remote(src, dst, send, recv, target):
    return pltpu.make_async_remote_copy(
        src_ref=src, dst_ref=dst, send_sem=send, recv_sem=recv, device_id=target, device_id_type=MESH
    )


def columns(h):
    return pl.ds(pl.multiple_of(h * DH, DH), DH)


def rows(at):
    return pl.ds(pl.multiple_of(at * ROWS, ROWS), ROWS)


def far_way(a, part):
    return 1 if (a + part) % 2 == 0 else -1


def x_first(a, part):
    return a == 0 and part != 4


def sides(a, part):
    return (0,) if x_first(a, part) else (1, 0)


def over_count(a, part):
    return NX if x_first(a, part) else 1


def part_count(a, g):
    return sum(g in sides(a, part) for part in range(NZ))


LONG1, LONG2, SHORT = 0, 1, 2


def fetch_kernel(
    sources, q_out, n_out, kv, cleared,
    tile_send, tile_recv, own_sem, x_send, x_recv, y_send, y_recv, pair_send, pair_recv,
    zeros, clear_sem,
):
    z, x, y, c = place()
    greet(z, x, y, c)
    side, odd = lax.div(y, 2), lax.rem(y, 2)
    xs = [around(x, dx, NX) for dx in range(NX)]
    other_y = beside(y)
    mine, theirs = half(y), half(other_y)
    to_x = {1: device(z, xs[1], y, c), -1: device(z, xs[-1], y, c)}
    to_y, to_core = device(z, x, NY - 1 - y, c), device(z, x, y, 1 - c)

    def tile_out(a, slot, turn):
        tz = around(z, -offset(slot), NZ)
        if a < 2:
            dst = kv.at[a, slot, x, c, side, rows(odd)]
        else:
            dst = (q_out, n_out)[a - 2].at[slot, rows(odd)]
        return remote(
            sources.at[a, :, columns(tz * 2 + (theirs if turn else mine))], dst, tile_send.at[a, turn],
            tile_recv.at[a, slot if a < 2 else turn], device(tz, x, other_y if turn else y, c),
        )

    def tiles(a, turn):
        slots = pl.ds(0, NZ - 1 + turn)
        if a < 2:
            ref = kv.at[a, slots, x, c, side, rows(0)]
        else:
            ref = (q_out, n_out)[a - 2].at[slots, rows(0)]
        return remote(ref, ref, tile_send.at[a, turn], tile_recv.at[a, turn], to_y)

    def tile_own(a):
        if a < 2:
            dst = kv.at[a, 0, x, c, side, rows(odd)]
        else:
            dst = (q_out, n_out)[a - 2].at[0, rows(odd)]
        return pltpu.make_async_copy(sources.at[a, :, columns(z * 2 + mine)], dst, own_sem.at[a])

    def send_tiles(first):
        for slot in range(NZ):
            for turn in (1, 0) if slot else (1,):
                for a in (first + 1, first):
                    tile_out(a, slot, turn).start()

    for a in (1, 0, 2, 3):
        tile_own(a).start()
    send_tiles(0)

    def chunk(a, part, dx, g):
        return kv.at[a, part, xs[dx % NX], c, side if g == 0 else 1 - side]

    def along_x(a, part, g, leg):
        way = far_way(a, part)
        dx, to = {LONG1: (0, way), LONG2: (-way, way), SHORT: (0, -way)}[leg]
        ref = chunk(a, part, dx, g)
        return remote(ref, ref, x_send.at[a, g, leg], x_recv.at[a, part, g, leg], to_x[to])

    def over_y(a, part, dx):
        ref = chunk(a, part, dx, 0)
        return remote(ref, ref, y_send.at[a, dx % NX], y_recv.at[a, part], to_y)

    def got_y(a, part):
        if x_first(a, part):
            ref = kv.at[a, part, :, c, 1 - side]
        else:
            ref = chunk(a, part, 0, 1)
        remote(ref, ref, y_send.at[a, 0], y_recv.at[a, part], to_y).wait_recv()

    def pair(a, part):
        ref = kv.at[a, part, :, c]
        return remote(ref, ref, pair_send.at[0], pair_recv.at[0], to_core)

    def entered(a, part):
        if part == 0:
            tile_own(a).wait()
            ref = kv.at[a, 0, x, c, side, rows(1 - odd)]
        else:
            ref = chunk(a, part, 0, 0)
        remote(ref, ref, tile_send.at[a, 1], tile_recv.at[a, part], to_y).wait_recv()

    def got_x(a, part, g, leg):
        way = far_way(a, part)
        dx = {LONG1: -way, LONG2: -2 * way, SHORT: way}[leg]
        ref = chunk(a, part, dx, g)
        remote(ref, ref, x_send.at[a, g, leg], x_recv.at[a, part, g, leg], to_y).wait_recv()
        if leg == LONG1:
            along_x(a, part, g, LONG2).start()
        if x_first(a, part):
            over_y(a, part, dx).start()

    def stage_a(part):
        for a in (1, 0):
            entered(a, part)
            over_y(a, part, 0).start()
            along_x(a, part, 0, LONG1).start()
            along_x(a, part, 0, SHORT).start()

    def stage_b(part):
        for a in (1, 0):
            if not x_first(a, part):
                got_y(a, part)
                along_x(a, part, 1, LONG1).start()
                along_x(a, part, 1, SHORT).start()
        for a in (0, 1):
            got_x(a, part, 0, LONG1)
            got_x(a, part, 0, SHORT)

    def stage_c(part):
        for a in (1, 0):
            if not x_first(a, part):
                got_x(a, part, 1, LONG1)
                got_x(a, part, 1, SHORT)
        got_x(0, part, 0, LONG2)
        got_x(1, part, 0, LONG2)

    def stage_d(part):
        for a in (1, 0):
            if x_first(a, part):
                got_y(a, part)
            else:
                got_x(a, part, 1, LONG2)
            pair(a, part).start()

    stages = (stage_a, stage_b, stage_c, stage_d)
    for time in range(NZ + len(stages) - 1):
        for late, stage in enumerate(stages):
            if 0 <= time - late < NZ:
                stage(time - late)
        if time == 0:
            zeros[...] = jnp.zeros(zeros.shape, jnp.bfloat16)
            for a in range(2):
                for i in range(NB // 64):
                    pltpu.make_async_copy(
                        zeros, cleared.at[a, pl.ds(i * 64, 64)], clear_sem.at[0]
                    ).start()
        if time == 4:
            send_tiles(2)

    pltpu.make_async_copy(cleared, cleared, clear_sem.at[0]).wait()
    for a in (2, 3):
        tile_own(a).wait()
    for a in range(4):
        for turn in range(2):
            tiles(a, turn).wait_send()
            if a >= 2:
                tiles(a, turn).wait_recv()
    for a in range(2):
        for g in range(2):
            if count := part_count(a, g):
                ref = kv.at[a, pl.ds(0, count), x, c, side]
                for leg in range(3):
                    remote(ref, ref, x_send.at[a, g, leg], x_recv.at[a, 0, g, leg], to_y).wait_send()
        for dx in range(NX):
            if count := sum(dx < over_count(a, part) for part in range(NZ)):
                ref = kv.at[a, pl.ds(0, count), x, c, side]
                remote(ref, ref, y_send.at[a, dx], y_recv.at[a, 0], to_y).wait_send()
    ref = kv.at[:, :, :, c]
    remote(ref, ref, pair_send.at[0], pair_recv.at[0], to_core).wait_send()
    ref = kv.at[:, :, :, 1 - c]
    remote(ref, ref, pair_send.at[0], pair_recv.at[0], to_core).wait_recv()


def attend_kernel(random_blocks, global_blocks, q, n, kv, cleared, att, dq, acc, global_sum):
    scaling = 1.0 / math.sqrt(DH)
    z, x, y, c = place()
    side = y // 2
    global_sum[...] = jnp.zeros(global_sum.shape, jnp.float32)
    column = lax.broadcasted_iota(jnp.int32, (1, ENTRIES * BLK), 1) // BLK

    def lies(block):
        away = ((block >> 6) - z) & (NZ - 1)
        slot = jnp.where(away <= NZ // 2, jnp.maximum(2 * away - 1, 0), 2 * (NZ - away))
        return slot * 64 + (block & 63)

    def dot(a, b, dims):
        return lax.dot_general(a, b, (dims, ((), ())), preferred_element_type=jnp.float32)

    globals_at = [lies(global_blocks[e]) for e in range(2)]

    def add(a, at, term):
        acc[a, at] = (acc[a, at].astype(jnp.float32) + term).astype(jnp.bfloat16)

    def group(g, carry):
        ids = [g * GROUP + u for u in range(GROUP)]
        blocks, entries = [], []
        for u in range(GROUP):
            plane = (z + offset(g * (GROUP // 4) + u // 4)) & (NZ - 1)
            block = ((plane * NX + x) * NC + c) * PER + side * 4 + u % 4
            blocks.append(block)
            near = [jnp.maximum(block - 1, 0), block, jnp.minimum(block + 1, NB - 1)]
            near += [random_blocks[e, block] for e in range(3)]
            entries.append([lies(b) for b in near] + globals_at)
        qs = [q[i] for i in ids]
        ks = [jnp.concatenate([kv[0, e] for e in es], 0) for es in entries]
        scores = [dot(a, b, ((1,), (1,))) * scaling for a, b in zip(qs, ks)]
        masked = []
        for u, (block, s) in enumerate(zip(blocks, scores)):
            if u % 4 == 0:
                s = jnp.where((column == 0) & (block == 0), -jnp.inf, s)
            if u % 4 == 3:
                s = jnp.where((column == 2) & (block == NB - 1), -jnp.inf, s)
            masked.append(s)
        raws = [jnp.exp(s - jnp.max(s, 1, keepdims=True)) for s in masked]
        probs = [r * (1.0 / jnp.sum(r, 1, keepdims=True)) for r in raws]
        probs_bf = [p.astype(jnp.bfloat16) for p in probs]
        vs = [jnp.concatenate([kv[1, e] for e in es], 0) for es in entries]
        atts = [dot(p, b, ((1,), (0,))).astype(jnp.bfloat16) for p, b in zip(probs_bf, vs)]
        grads = []
        for i, a in zip(ids, atts):
            att[i] = a
            grads.append((a.astype(jnp.float32) - n[i].astype(jnp.float32)).astype(jnp.bfloat16))
        dprobs = [dot(d, b, ((1,), (1,))) for d, b in zip(grads, vs)]
        dscores = [
            (p * (d - jnp.sum(p * d, 1, keepdims=True))).astype(jnp.bfloat16)
            for p, d in zip(probs, dprobs)
        ]
        for i, d, b in zip(ids, dscores, ks):
            dq[i] = (dot(d, b, ((1,), (0,))) * scaling).astype(jnp.bfloat16)
        terms = (
            [dot(d, a, ((0,), (0,))) * scaling for d, a in zip(dscores, qs)],
            [dot(p, d, ((0,), (0,))) for p, d in zip(probs_bf, grads)],
        )

        for a in range(2):
            def term(u, e):
                return terms[a][u][e * BLK : (e + 1) * BLK]

            for first in range(0, GROUP, 4):
                last = first + 3
                add(a, entries[first][0], term(first, 0))
                for u in range(first, last + 1):
                    total = term(u, 1)
                    if u > first:
                        total += term(u - 1, 2)
                    if u < last:
                        total += term(u + 1, 0)
                    add(a, entries[u][1], total)
                add(a, entries[last][2], term(last, 2))
            for u in range(GROUP):
                for e in range(3, 6):
                    add(a, entries[u][e], term(u, e))
            for e in range(2):
                global_sum[a, e] += sum(term(u, 6 + e) for u in range(GROUP))
        return carry

    lax.fori_loop(0, QUERIES // GROUP, group, 0)
    for a in range(2):
        for e in range(2):
            add(a, globals_at[e], global_sum[a, e])


def return_kernel(
    att, dq, partial, att_out, dq_out, dk_out, dv_out,
    own, sib, x_came, y_came, pair_send, pair_recv, x_send, x_recv, y_send, y_recv,
    tile_send, tile_recv, tile_sem,
):
    z, x, y, c = place()
    greet(z, x, y, c)
    side, odd = lax.div(y, 2), lax.rem(y, 2)
    xs = [around(x, dx, NX) for dx in range(NX)]
    other_y = beside(y)
    to_x = {1: device(z, xs[1], y, c), -1: device(z, xs[-1], y, c)}
    to_y, to_core = device(z, x, NY - 1 - y, c), device(z, x, y, 1 - c)
    head = columns(z * 2 + half(y))

    def pair(a, part):
        return remote(
            partial.at[a, part, :, 1 - c], sib.at[a, part], pair_send.at[0], pair_recv.at[a, part],
            to_core,
        )

    order = tuple(reversed(range(NZ)))
    for part in order:
        for a in (0, 1):
            pair(a, part).start()

    outs = (dk_out, dv_out, att_out, dq_out)

    def source(a, slots, row):
        if a < 2:
            return own.at[a, slots, x, side, rows(row)]
        return (att, dq)[a - 2].at[slots, rows(row)]

    def tile_out(a, slot, turn):
        return remote(
            source(a, slot, 1 - odd if turn else odd), outs[a].at[:, head], tile_send.at[a, turn],
            tile_recv.at[a, turn], device(around(z, offset(slot), NZ), x, other_y if turn else y, c),
        )

    def tiles(a, turn):
        count = NZ - 1 + turn
        return remote(
            source(a, pl.ds(0, count), 0), outs[a].at[:, pl.ds(0, count * DH)], tile_send.at[a, turn],
            tile_recv.at[a, turn], to_y,
        )

    def tile_own(a):
        return pltpu.make_async_copy(source(a, 0, odd), outs[a].at[:, head], tile_sem.at[a])

    def send_tiles(a, part):
        for turn in range(2):
            if part == 0 and turn == 0:
                tile_own(a).start()
            else:
                tile_out(a, part, turn).start()

    def sum_up(a, part, dx, g, first, came):
        at_x, gs = xs[dx % NX], side if g == 0 else 1 - side
        if first:
            total = partial[a, part, at_x, c, gs].astype(jnp.float32)
            total += sib[a, part, at_x, gs].astype(jnp.float32)
        else:
            total = own[a, part, at_x, gs].astype(jnp.float32)
        for ref in came:
            total += ref[...].astype(jnp.float32)
        own[a, part, at_x, gs] = total.astype(jnp.bfloat16)

    def chunk(a, part, dx, g):
        return own.at[a, part, xs[dx % NX], side if g == 0 else 1 - side]

    def landed_x(a, part, g, leg):
        return x_came.at[2 * a + g, part, leg]

    def landed_y(a, part, dx):
        return y_came.at[part, dx % NX if a == 0 else NX]

    def along_x(a, part, g, leg):
        way = far_way(a, part)
        dx, to = {LONG1: (2 * way, way), LONG2: (way, way), SHORT: (-way, -way)}[leg]
        return remote(
            chunk(a, part, dx, g), landed_x(a, part, g, leg), x_send.at[a, g, leg],
            x_recv.at[a, part, g, leg], to_x[to],
        )

    def over_y(a, part, dx):
        return remote(
            chunk(a, part, dx, 1), landed_y(a, part, dx), y_send.at[a, dx % NX],
            y_recv.at[a, part, dx % NX], to_y,
        )

    def leg(a, part, g, dx, name, came):
        if x_first(a, part):
            over_y(a, part, dx).wait_recv()
            came = came + [landed_y(a, part, dx)]
        sum_up(a, part, dx, g, True, came)
        along_x(a, part, g, name).start()

    def first_legs(a, part):
        way = far_way(a, part)
        for g in sides(a, part):
            leg(a, part, g, 2 * way, LONG1, [])
            leg(a, part, g, -way, SHORT, [])

    def last_sum(a, part, g):
        along_x(a, part, g, LONG2).wait_recv()
        along_x(a, part, g, SHORT).wait_recv()
        came = [landed_x(a, part, g, LONG2), landed_x(a, part, g, SHORT)]
        if x_first(a, part):
            over_y(a, part, 0).wait_recv()
            came = came + [landed_y(a, part, 0)]
        sum_up(a, part, 0, g, True, came)

    def begin(part):
        for a in range(2):
            pair(a, part).wait_recv()
            if x_first(a, part):
                way = far_way(a, part)
                for dx in (2 * way, -way, way, 0):
                    sum_up(a, part, dx, 1, True, [])
                    over_y(a, part, dx).start()
            else:
                first_legs(a, part)

    def after_y(part):
        for a in range(2):
            if x_first(a, part):
                first_legs(a, part)

    def seconds(part):
        for a in (1, 0):
            for g in sides(a, part):
                along_x(a, part, g, LONG1).wait_recv()
                leg(a, part, g, far_way(a, part), LONG2, [landed_x(a, part, g, LONG1)])

    def over(part):
        for a in (1, 0):
            if not x_first(a, part):
                last_sum(a, part, 1)
                over_y(a, part, 0).start()

    def lasts(part):
        for a in range(2):
            last_sum(a, part, 0)
            if not x_first(a, part):
                over_y(a, part, 0).wait_recv()
                sum_up(a, part, 0, 0, False, [landed_y(a, part, 0)])
            send_tiles(a, part)

    for part in order:
        for a in (2, 3):
            send_tiles(a, part)

    plan = ((after_y, 1), (begin, 0), (seconds, 2), (over, 3), (lasts, 4))
    for time in range(NZ + 4):
        for stage, late in plan:
            if 0 <= time - late < NZ:
                stage(order[time - late])

    for a in range(4):
        tile_own(a).wait()
        for turn in range(2):
            tiles(a, turn).wait_send()
            tiles(a, turn).wait_recv()
    for a in range(2):
        for g in range(2):
            if count := part_count(a, g):
                ref = own.at[a, pl.ds(0, count), x, side]
                for name in range(3):
                    remote(ref, ref, x_send.at[a, g, name], x_recv.at[a, 0, g, name], to_y).wait_send()
        for dx in range(NX):
            if count := sum(dx < over_count(a, part) for part in range(NZ)):
                ref = own.at[a, pl.ds(0, count), x, side]
                remote(ref, ref, y_send.at[a, dx], y_recv.at[a, 0, dx], to_y).wait_send()
    remote(
        partial.at[:, :, :, 1 - c], sib, pair_send.at[0], pair_recv.at[0, 0], to_core
    ).wait_send()


def write_kernel(*refs):
    moves = [pltpu.make_async_copy(refs[i], refs[4 + i], refs[8].at[i]) for i in range(4)]
    for move in moves:
        move.start()
    for move in moves:
        move.wait()


ANY = pl.BlockSpec(memory_space=pl.ANY)
VMEM = pl.BlockSpec(memory_space=pltpu.VMEM)
SMEM = pl.BlockSpec(memory_space=pltpu.SMEM)
DMA = pltpu.SemaphoreType.DMA


def bf16(*shape):
    return jax.ShapeDtypeStruct(shape, jnp.bfloat16)


def copies(*shape):
    return [DMA(shape), DMA(shape)]


def shards(queries, keys, values, noise, random_blocks, global_blocks):
    gathered = (2, NZ, NX, NC, 2, SIDE, DH)
    q_all, n_all, kv, cleared = pl.pallas_call(
        fetch_kernel,
        name="fetch",
        out_shape=(
            bf16(NZ, SIDE, DH), bf16(NZ, SIDE, DH), bf16(*gathered), bf16(2, NB, BLK, DH)
        ),
        in_specs=[ANY],
        out_specs=(ANY, ANY, ANY, ANY),
        scratch_shapes=[
            DMA((4, 2)), DMA((4, NZ)), DMA((4,)), DMA((2, 2, 3)), DMA((2, NZ, 2, 3)),
            DMA((2, NX)), DMA((2, NZ)), *copies(1), pltpu.VMEM((64, BLK, DH), jnp.bfloat16), DMA((1,)),
        ],
        cost_estimate=pl.CostEstimate(flops=8 * 10**10, bytes_accessed=1, transcendentals=0),
        compiler_params=pltpu.CompilerParams(
            collective_id=0, has_side_effects=True, vmem_limit_bytes=FETCH_MIB * 2**20
        ),
    )(jnp.stack([keys, values, queries, noise]))

    att, dq, partial = pl.pallas_call(
        attend_kernel,
        name="attend",
        out_shape=(bf16(QUERIES, BLK, DH), bf16(QUERIES, BLK, DH), bf16(2, NB, BLK, DH)),
        in_specs=[SMEM, SMEM, VMEM, VMEM, VMEM, VMEM],
        out_specs=(VMEM, VMEM, VMEM),
        scratch_shapes=[pltpu.VMEM((2, 2, BLK, DH), jnp.float32)],
        input_output_aliases={5: 2},
        compiler_params=pltpu.CompilerParams(vmem_limit_bytes=ATTEND_MIB * 2**20),
    )(
        random_blocks.T, global_blocks, q_all.reshape(QUERIES, BLK, DH),
        n_all.reshape(QUERIES, BLK, DH), kv.reshape(2, NB, BLK, DH), cleared,
    )

    outs = pl.pallas_call(
        return_kernel,
        name="give_back",
        out_shape=(bf16(ROWS, HEADS * DH),) * 4,
        in_specs=[ANY, ANY, VMEM],
        out_specs=(ANY,) * 4,
        scratch_shapes=[
            pltpu.VMEM((2, NZ, NX, 2, SIDE, DH), jnp.bfloat16),
            pltpu.VMEM((2, NZ, NX, 2, SIDE, DH), jnp.bfloat16),
            pltpu.VMEM((4, NZ, 3, SIDE, DH), jnp.bfloat16),
            pltpu.VMEM((NZ, NX + 1, SIDE, DH), jnp.bfloat16),
            DMA((1,)), DMA((2, NZ)), DMA((2, 2, 3)), DMA((2, NZ, 2, 3)), DMA((2, NX)),
            DMA((2, NZ, NX)), *copies(4, 2), DMA((4,)),
        ],
        compiler_params=pltpu.CompilerParams(
            collective_id=1, has_side_effects=True, vmem_limit_bytes=RETURN_MIB * 2**20
        ),
    )(att.reshape(NZ, SIDE, DH), dq.reshape(NZ, SIDE, DH), partial.reshape(gathered))
    return pl.pallas_call(
        write_kernel,
        name="write",
        out_shape=(bf16(ROWS, HEADS * DH),) * 4,
        in_specs=[VMEM] * 4,
        out_specs=(ANY,) * 4,
        scratch_shapes=[DMA((4,))],
        compiler_params=pltpu.CompilerParams(vmem_limit_bytes=2**20),
    )(*outs)


def solution(mesh):
    rows = P(("seq", "head"), None)
    return jax.shard_map(
        shards,
        mesh=mesh,
        in_specs=(rows, rows, rows, rows, P(), P()),
        out_specs=(rows, rows, rows, rows),
        check_vma=False,
    )
```

```python
import math

import jax
import jax.numpy as jnp
from jax import lax
from jax.experimental import pallas as pl
from jax.experimental.pallas import tpu as pltpu
from jax.sharding import PartitionSpec as P

DH = 128
BLK = 64
NX, NY, NZ, NC = 4, 4, 8, 2
ROWS = 128
SIDE = 2 * ROWS
SHARD = NY * ROWS
PER = SHARD // BLK
NB = NZ * NX * NC * PER
QUERIES = NZ * SIDE // BLK
HEADS = 16
ENTRIES = 8
GROUP = 16
FETCH_MIB, ATTEND_MIB, RETURN_MIB = 4, 8, 26
MESH = pl.DeviceIdType.MESH


def place():
    seq, y = lax.axis_index("seq"), lax.axis_index("head")
    return lax.div(seq, NX * NC), lax.rem(lax.div(seq, NC), NX), y, lax.rem(seq, NC)


def device(z, x, y, c):
    return ((z * NX + x) * NC + c, y)


def around(base, step, count):
    return lax.rem(base + step % count, count)


def offset(slot):
    return (slot + 1) // 2 * (2 * (slot % 2) - 1)


def beside(y):
    return y + 1 - 2 * lax.rem(y, 2)


def half(y):
    return lax.rem(lax.div(y + 1, 2), 2)


def greet(z, x, y, c):
    barrier = pltpu.get_barrier_semaphore()

    def signal(target):
        pl.semaphore_signal(barrier, inc=1, device_id=target, device_id_type=MESH)

    for dz in range(1, NZ):
        signal(device(around(z, dz, NZ), x, y, c))
        signal(device(around(z, dz, NZ), x, beside(y), c))
    signal(device(z, x, beside(y), c))
    signal(device(z, around(x, 1, NX), y, c))
    signal(device(z, around(x, -1, NX), y, c))
    signal(device(z, x, NY - 1 - y, c))
    signal(device(z, x, y, 1 - c))
    pl.semaphore_wait(barrier, 2 * NZ - 1 + 4)


def remote(src, dst, send, recv, target):
    return pltpu.make_async_remote_copy(
        src_ref=src, dst_ref=dst, send_sem=send, recv_sem=recv, device_id=target, device_id_type=MESH
    )


def columns(h):
    return pl.ds(pl.multiple_of(h * DH, DH), DH)


def rows(at):
    return pl.ds(pl.multiple_of(at * ROWS, ROWS), ROWS)


def far_way(a, part):
    return 1 if (a + part) % 2 == 0 else -1


def x_first(a, part):
    return a == 0 and part != 4


def sides(a, part):
    return (0,) if x_first(a, part) else (1, 0)


def over_count(a, part):
    return NX if x_first(a, part) else 1


def part_count(a, g):
    return sum(g in sides(a, part) for part in range(NZ))


LONG1, LONG2, SHORT = 0, 1, 2


def fetch_kernel(
    sources, q_out, n_out, kv, cleared,
    tile_send, tile_recv, own_sem, x_send, x_recv, y_send, y_recv, pair_send, pair_recv,
    zeros, clear_sem,
):
    z, x, y, c = place()
    greet(z, x, y, c)
    side, odd = lax.div(y, 2), lax.rem(y, 2)
    xs = [around(x, dx, NX) for dx in range(NX)]
    other_y = beside(y)
    mine, theirs = half(y), half(other_y)
    to_x = {1: device(z, xs[1], y, c), -1: device(z, xs[-1], y, c)}
    to_y, to_core = device(z, x, NY - 1 - y, c), device(z, x, y, 1 - c)

    def tile_out(a, slot, turn):
        tz = around(z, -offset(slot), NZ)
        if a < 2:
            dst = kv.at[a, slot, x, c, side, rows(odd)]
        else:
            dst = (q_out, n_out)[a - 2].at[slot, rows(odd)]
        return remote(
            sources.at[a, :, columns(tz * 2 + (theirs if turn else mine))], dst, tile_send.at[a, turn],
            tile_recv.at[a, slot if a < 2 else turn], device(tz, x, other_y if turn else y, c),
        )

    def tiles(a, turn):
        slots = pl.ds(0, NZ - 1 + turn)
        if a < 2:
            ref = kv.at[a, slots, x, c, side, rows(0)]
        else:
            ref = (q_out, n_out)[a - 2].at[slots, rows(0)]
        return remote(ref, ref, tile_send.at[a, turn], tile_recv.at[a, turn], to_y)

    def tile_own(a):
        if a < 2:
            dst = kv.at[a, 0, x, c, side, rows(odd)]
        else:
            dst = (q_out, n_out)[a - 2].at[0, rows(odd)]
        return pltpu.make_async_copy(sources.at[a, :, columns(z * 2 + mine)], dst, own_sem.at[a])

    def send_tiles(first, slots):
        for slot in slots:
            for turn in (1, 0) if slot else (1,):
                for a in (first + 1, first):
                    tile_out(a, slot, turn).start()

    for a in (1, 0, 2, 3):
        tile_own(a).start()
    send_tiles(0, range(3))

    def chunk(a, part, dx, g):
        return kv.at[a, part, xs[dx % NX], c, side if g == 0 else 1 - side]

    def along_x(a, part, g, leg):
        way = far_way(a, part)
        dx, to = {LONG1: (0, way), LONG2: (-way, way), SHORT: (0, -way)}[leg]
        ref = chunk(a, part, dx, g)
        return remote(ref, ref, x_send.at[a, g, leg], x_recv.at[a, part, g, leg], to_x[to])

    def over_y(a, part, dx):
        ref = chunk(a, part, dx, 0)
        return remote(ref, ref, y_send.at[a, dx % NX], y_recv.at[a, part], to_y)

    def got_y(a, part):
        if x_first(a, part):
            ref = kv.at[a, part, :, c, 1 - side]
        else:
            ref = chunk(a, part, 0, 1)
        remote(ref, ref, y_send.at[a, 0], y_recv.at[a, part], to_y).wait_recv()

    def pair(a, part):
        ref = kv.at[a, part, :, c]
        return remote(ref, ref, pair_send.at[0], pair_recv.at[0], to_core)

    def entered(a, part):
        if part == 0:
            tile_own(a).wait()
            ref = kv.at[a, 0, x, c, side, rows(1 - odd)]
        else:
            ref = chunk(a, part, 0, 0)
        remote(ref, ref, tile_send.at[a, 1], tile_recv.at[a, part], to_y).wait_recv()

    def got_x(a, part, g, leg):
        way = far_way(a, part)
        dx = {LONG1: -way, LONG2: -2 * way, SHORT: way}[leg]
        ref = chunk(a, part, dx, g)
        remote(ref, ref, x_send.at[a, g, leg], x_recv.at[a, part, g, leg], to_y).wait_recv()
        if leg == LONG1:
            along_x(a, part, g, LONG2).start()
        if x_first(a, part):
            over_y(a, part, dx).start()

    def stage_a(part):
        for a in (1, 0):
            entered(a, part)
            over_y(a, part, 0).start()
            along_x(a, part, 0, LONG1).start()
            along_x(a, part, 0, SHORT).start()

    def stage_b(part):
        for a in (1, 0):
            if not x_first(a, part):
                got_y(a, part)
                along_x(a, part, 1, LONG1).start()
                along_x(a, part, 1, SHORT).start()
        for a in (0, 1):
            got_x(a, part, 0, LONG1)
            got_x(a, part, 0, SHORT)

    def stage_c(part):
        for a in (1, 0):
            if not x_first(a, part):
                got_x(a, part, 1, LONG1)
                got_x(a, part, 1, SHORT)
        got_x(0, part, 0, LONG2)
        got_x(1, part, 0, LONG2)

    def stage_d(part):
        for a in (1, 0):
            if x_first(a, part):
                got_y(a, part)
            else:
                got_x(a, part, 1, LONG2)
            pair(a, part).start()

    stages = (stage_a, stage_b, stage_c, stage_d)
    for time in range(NZ + len(stages) - 1):
        for late, stage in enumerate(stages):
            if 0 <= time - late < NZ:
                stage(time - late)
        if time == 0:
            send_tiles(0, range(3, NZ))
        if time == 2:
            zeros[...] = jnp.zeros(zeros.shape, jnp.bfloat16)
            for a in range(2):
                for i in range(NB // 64):
                    pltpu.make_async_copy(
                        zeros, cleared.at[a, pl.ds(i * 64, 64)], clear_sem.at[0]
                    ).start()
        if 3 <= time < 3 + NZ // 2:
            send_tiles(2, (2 * time - 6, 2 * time - 5))

    pltpu.make_async_copy(cleared, cleared, clear_sem.at[0]).wait()
    for a in (2, 3):
        tile_own(a).wait()
    for a in range(4):
        for turn in range(2):
            tiles(a, turn).wait_send()
            if a >= 2:
                tiles(a, turn).wait_recv()
    for a in range(2):
        for g in range(2):
            if count := part_count(a, g):
                ref = kv.at[a, pl.ds(0, count), x, c, side]
                for leg in range(3):
                    remote(ref, ref, x_send.at[a, g, leg], x_recv.at[a, 0, g, leg], to_y).wait_send()
        for dx in range(NX):
            if count := sum(dx < over_count(a, part) for part in range(NZ)):
                ref = kv.at[a, pl.ds(0, count), x, c, side]
                remote(ref, ref, y_send.at[a, dx], y_recv.at[a, 0], to_y).wait_send()
    ref = kv.at[:, :, :, c]
    remote(ref, ref, pair_send.at[0], pair_recv.at[0], to_core).wait_send()
    ref = kv.at[:, :, :, 1 - c]
    remote(ref, ref, pair_send.at[0], pair_recv.at[0], to_core).wait_recv()


def attend_kernel(random_blocks, global_blocks, q, n, kv, cleared, att, dq, acc, global_sum):
    scaling = 1.0 / math.sqrt(DH)
    z, x, y, c = place()
    side = y // 2
    global_sum[...] = jnp.zeros(global_sum.shape, jnp.float32)
    column = lax.broadcasted_iota(jnp.int32, (1, ENTRIES * BLK), 1) // BLK

    def lies(block):
        away = ((block >> 6) - z) & (NZ - 1)
        slot = jnp.where(away <= NZ // 2, jnp.maximum(2 * away - 1, 0), 2 * (NZ - away))
        return slot * 64 + (block & 63)

    def dot(a, b, dims):
        return lax.dot_general(a, b, (dims, ((), ())), preferred_element_type=jnp.float32)

    globals_at = [lies(global_blocks[e]) for e in range(2)]

    def add(a, at, term):
        acc[a, at] = (acc[a, at].astype(jnp.float32) + term).astype(jnp.bfloat16)

    def group(g, carry):
        ids = [g * GROUP + u for u in range(GROUP)]
        blocks, entries = [], []
        for u in range(GROUP):
            plane = (z + offset(g * (GROUP // 4) + u // 4)) & (NZ - 1)
            block = ((plane * NX + x) * NC + c) * PER + side * 4 + u % 4
            blocks.append(block)
            near = [jnp.maximum(block - 1, 0), block, jnp.minimum(block + 1, NB - 1)]
            near += [random_blocks[e, block] for e in range(3)]
            entries.append([lies(b) for b in near] + globals_at)
        qs = [q[i] for i in ids]
        ks = [jnp.concatenate([kv[0, e] for e in es], 0) for es in entries]
        scores = [dot(a, b, ((1,), (1,))) * scaling for a, b in zip(qs, ks)]
        masked = []
        for u, (block, s) in enumerate(zip(blocks, scores)):
            if u % 4 == 0:
                s = jnp.where((column == 0) & (block == 0), -jnp.inf, s)
            if u % 4 == 3:
                s = jnp.where((column == 2) & (block == NB - 1), -jnp.inf, s)
            masked.append(s)
        raws = [jnp.exp(s - jnp.max(s, 1, keepdims=True)) for s in masked]
        probs = [r * (1.0 / jnp.sum(r, 1, keepdims=True)) for r in raws]
        probs_bf = [p.astype(jnp.bfloat16) for p in probs]
        vs = [jnp.concatenate([kv[1, e] for e in es], 0) for es in entries]
        atts = [dot(p, b, ((1,), (0,))).astype(jnp.bfloat16) for p, b in zip(probs_bf, vs)]
        grads = []
        for i, a in zip(ids, atts):
            att[i] = a
            grads.append((a.astype(jnp.float32) - n[i].astype(jnp.float32)).astype(jnp.bfloat16))
        dprobs = [dot(d, b, ((1,), (1,))) for d, b in zip(grads, vs)]
        dscores = [
            (p * (d - jnp.sum(p * d, 1, keepdims=True))).astype(jnp.bfloat16)
            for p, d in zip(probs, dprobs)
        ]
        for i, d, b in zip(ids, dscores, ks):
            dq[i] = (dot(d, b, ((1,), (0,))) * scaling).astype(jnp.bfloat16)
        terms = (
            [dot(d, a, ((0,), (0,))) * scaling for d, a in zip(dscores, qs)],
            [dot(p, d, ((0,), (0,))) for p, d in zip(probs_bf, grads)],
        )

        for a in range(2):
            def term(u, e):
                return terms[a][u][e * BLK : (e + 1) * BLK]

            for first in range(0, GROUP, 4):
                last = first + 3
                add(a, entries[first][0], term(first, 0))
                for u in range(first, last + 1):
                    total = term(u, 1)
                    if u > first:
                        total += term(u - 1, 2)
                    if u < last:
                        total += term(u + 1, 0)
                    add(a, entries[u][1], total)
                add(a, entries[last][2], term(last, 2))
            for u in range(GROUP):
                for e in range(3, 6):
                    add(a, entries[u][e], term(u, e))
            for e in range(2):
                global_sum[a, e] += sum(term(u, 6 + e) for u in range(GROUP))
        return carry

    lax.fori_loop(0, QUERIES // GROUP, group, 0)
    for a in range(2):
        for e in range(2):
            add(a, globals_at[e], global_sum[a, e])


def return_kernel(
    att, dq, partial, att_out, dq_out, dk_out, dv_out,
    own, sib, x_came, y_came, pair_send, pair_recv, x_send, x_recv, y_send, y_recv,
    tile_send, tile_recv, tile_sem,
):
    z, x, y, c = place()
    greet(z, x, y, c)
    side, odd = lax.div(y, 2), lax.rem(y, 2)
    xs = [around(x, dx, NX) for dx in range(NX)]
    other_y = beside(y)
    to_x = {1: device(z, xs[1], y, c), -1: device(z, xs[-1], y, c)}
    to_y, to_core = device(z, x, NY - 1 - y, c), device(z, x, y, 1 - c)
    head = columns(z * 2 + half(y))

    def pair(a, part):
        return remote(
            partial.at[a, part, :, 1 - c], sib.at[a, part], pair_send.at[0], pair_recv.at[a, part],
            to_core,
        )

    order = tuple(reversed(range(NZ)))
    for part in order:
        for a in (0, 1):
            pair(a, part).start()

    outs = (dk_out, dv_out, att_out, dq_out)

    def source(a, slots, row):
        if a < 2:
            return own.at[a, slots, x, side, rows(row)]
        return (att, dq)[a - 2].at[slots, rows(row)]

    def tile_out(a, slot, turn):
        return remote(
            source(a, slot, 1 - odd if turn else odd), outs[a].at[:, head], tile_send.at[a, turn],
            tile_recv.at[a, turn], device(around(z, offset(slot), NZ), x, other_y if turn else y, c),
        )

    def tiles(a, turn):
        count = NZ - 1 + turn
        return remote(
            source(a, pl.ds(0, count), 0), outs[a].at[:, pl.ds(0, count * DH)], tile_send.at[a, turn],
            tile_recv.at[a, turn], to_y,
        )

    def tile_own(a):
        return pltpu.make_async_copy(source(a, 0, odd), outs[a].at[:, head], tile_sem.at[a])

    def send_tiles(a, part):
        for turn in range(2):
            if part == 0 and turn == 0:
                tile_own(a).start()
            else:
                tile_out(a, part, turn).start()

    def sum_up(a, part, dx, g, first, came):
        at_x, gs = xs[dx % NX], side if g == 0 else 1 - side
        if first:
            total = partial[a, part, at_x, c, gs].astype(jnp.float32)
            total += sib[a, part, at_x, gs].astype(jnp.float32)
        else:
            total = own[a, part, at_x, gs].astype(jnp.float32)
        for ref in came:
            total += ref[...].astype(jnp.float32)
        own[a, part, at_x, gs] = total.astype(jnp.bfloat16)

    def chunk(a, part, dx, g):
        return own.at[a, part, xs[dx % NX], side if g == 0 else 1 - side]

    def landed_x(a, part, g, leg):
        return x_came.at[2 * a + g, part, leg]

    def landed_y(a, part, dx):
        return y_came.at[part, dx % NX if a == 0 else NX]

    def along_x(a, part, g, leg):
        way = far_way(a, part)
        dx, to = {LONG1: (2 * way, way), LONG2: (way, way), SHORT: (-way, -way)}[leg]
        return remote(
            chunk(a, part, dx, g), landed_x(a, part, g, leg), x_send.at[a, g, leg],
            x_recv.at[a, part, g, leg], to_x[to],
        )

    def over_y(a, part, dx):
        return remote(
            chunk(a, part, dx, 1), landed_y(a, part, dx), y_send.at[a, dx % NX],
            y_recv.at[a, part, dx % NX], to_y,
        )

    def leg(a, part, g, dx, name, came):
        if x_first(a, part):
            over_y(a, part, dx).wait_recv()
            came = came + [landed_y(a, part, dx)]
        sum_up(a, part, dx, g, True, came)
        along_x(a, part, g, name).start()

    def first_legs(a, part):
        way = far_way(a, part)
        for g in sides(a, part):
            leg(a, part, g, 2 * way, LONG1, [])
            leg(a, part, g, -way, SHORT, [])

    def last_sum(a, part, g):
        along_x(a, part, g, LONG2).wait_recv()
        along_x(a, part, g, SHORT).wait_recv()
        came = [landed_x(a, part, g, LONG2), landed_x(a, part, g, SHORT)]
        if x_first(a, part):
            over_y(a, part, 0).wait_recv()
            came = came + [landed_y(a, part, 0)]
        sum_up(a, part, 0, g, True, came)

    def begin(part):
        for a in range(2):
            pair(a, part).wait_recv()
            if x_first(a, part):
                way = far_way(a, part)
                for dx in (2 * way, -way, way, 0):
                    sum_up(a, part, dx, 1, True, [])
                    over_y(a, part, dx).start()
            else:
                first_legs(a, part)

    def after_y(part):
        for a in range(2):
            if x_first(a, part):
                first_legs(a, part)

    def seconds(part):
        for a in (1, 0):
            for g in sides(a, part):
                along_x(a, part, g, LONG1).wait_recv()
                leg(a, part, g, far_way(a, part), LONG2, [landed_x(a, part, g, LONG1)])

    def over(part):
        for a in (1, 0):
            if not x_first(a, part):
                last_sum(a, part, 1)
                over_y(a, part, 0).start()

    def lasts(part):
        for a in range(2):
            last_sum(a, part, 0)
            if not x_first(a, part):
                over_y(a, part, 0).wait_recv()
                sum_up(a, part, 0, 0, False, [landed_y(a, part, 0)])
            send_tiles(a, part)

    plan = ((after_y, 1), (begin, 0), (seconds, 2), (over, 3), (lasts, 4))
    for time in range(NZ + 4):
        for stage, late in plan:
            if 0 <= time - late < NZ:
                stage(order[time - late])
        if time < NZ:
            for a in (2, 3):
                send_tiles(a, order[time])

    for a in range(4):
        tile_own(a).wait()
        for turn in range(2):
            tiles(a, turn).wait_send()
            tiles(a, turn).wait_recv()
    for a in range(2):
        for g in range(2):
            if count := part_count(a, g):
                ref = own.at[a, pl.ds(0, count), x, side]
                for name in range(3):
                    remote(ref, ref, x_send.at[a, g, name], x_recv.at[a, 0, g, name], to_y).wait_send()
        for dx in range(NX):
            if count := sum(dx < over_count(a, part) for part in range(NZ)):
                ref = own.at[a, pl.ds(0, count), x, side]
                remote(ref, ref, y_send.at[a, dx], y_recv.at[a, 0, dx], to_y).wait_send()
    remote(
        partial.at[:, :, :, 1 - c], sib, pair_send.at[0], pair_recv.at[0, 0], to_core
    ).wait_send()


def write_kernel(*refs):
    moves = [pltpu.make_async_copy(refs[i], refs[4 + i], refs[8].at[i]) for i in range(4)]
    for move in moves:
        move.start()
    for move in moves:
        move.wait()


ANY = pl.BlockSpec(memory_space=pl.ANY)
VMEM = pl.BlockSpec(memory_space=pltpu.VMEM)
SMEM = pl.BlockSpec(memory_space=pltpu.SMEM)
DMA = pltpu.SemaphoreType.DMA


def bf16(*shape):
    return jax.ShapeDtypeStruct(shape, jnp.bfloat16)


def copies(*shape):
    return [DMA(shape), DMA(shape)]


def shards(queries, keys, values, noise, random_blocks, global_blocks):
    gathered = (2, NZ, NX, NC, 2, SIDE, DH)
    q_all, n_all, kv, cleared = pl.pallas_call(
        fetch_kernel,
        name="fetch",
        out_shape=(
            bf16(NZ, SIDE, DH), bf16(NZ, SIDE, DH), bf16(*gathered), bf16(2, NB, BLK, DH)
        ),
        in_specs=[ANY],
        out_specs=(ANY, ANY, ANY, ANY),
        scratch_shapes=[
            DMA((4, 2)), DMA((4, NZ)), DMA((4,)), DMA((2, 2, 3)), DMA((2, NZ, 2, 3)),
            DMA((2, NX)), DMA((2, NZ)), *copies(1), pltpu.VMEM((64, BLK, DH), jnp.bfloat16), DMA((1,)),
        ],
        cost_estimate=pl.CostEstimate(flops=8 * 10**10, bytes_accessed=1, transcendentals=0),
        compiler_params=pltpu.CompilerParams(
            collective_id=0, has_side_effects=True, vmem_limit_bytes=FETCH_MIB * 2**20
        ),
    )(jnp.stack([keys, values, queries, noise]))

    att, dq, partial = pl.pallas_call(
        attend_kernel,
        name="attend",
        out_shape=(bf16(QUERIES, BLK, DH), bf16(QUERIES, BLK, DH), bf16(2, NB, BLK, DH)),
        in_specs=[SMEM, SMEM, VMEM, VMEM, VMEM, VMEM],
        out_specs=(VMEM, VMEM, VMEM),
        scratch_shapes=[pltpu.VMEM((2, 2, BLK, DH), jnp.float32)],
        input_output_aliases={5: 2},
        compiler_params=pltpu.CompilerParams(vmem_limit_bytes=ATTEND_MIB * 2**20),
    )(
        random_blocks.T, global_blocks, q_all.reshape(QUERIES, BLK, DH),
        n_all.reshape(QUERIES, BLK, DH), kv.reshape(2, NB, BLK, DH), cleared,
    )

    outs = pl.pallas_call(
        return_kernel,
        name="give_back",
        out_shape=(bf16(ROWS, HEADS * DH),) * 4,
        in_specs=[ANY, ANY, VMEM],
        out_specs=(ANY,) * 4,
        scratch_shapes=[
            pltpu.VMEM((2, NZ, NX, 2, SIDE, DH), jnp.bfloat16),
            pltpu.VMEM((2, NZ, NX, 2, SIDE, DH), jnp.bfloat16),
            pltpu.VMEM((4, NZ, 3, SIDE, DH), jnp.bfloat16),
            pltpu.VMEM((NZ, NX + 1, SIDE, DH), jnp.bfloat16),
            DMA((1,)), DMA((2, NZ)), DMA((2, 2, 3)), DMA((2, NZ, 2, 3)), DMA((2, NX)),
            DMA((2, NZ, NX)), *copies(4, 2), DMA((4,)),
        ],
        compiler_params=pltpu.CompilerParams(
            collective_id=1, has_side_effects=True, vmem_limit_bytes=RETURN_MIB * 2**20
        ),
    )(att.reshape(NZ, SIDE, DH), dq.reshape(NZ, SIDE, DH), partial.reshape(gathered))
    return pl.pallas_call(
        write_kernel,
        name="write",
        out_shape=(bf16(ROWS, HEADS * DH),) * 4,
        in_specs=[VMEM] * 4,
        out_specs=(ANY,) * 4,
        scratch_shapes=[DMA((4,))],
        compiler_params=pltpu.CompilerParams(vmem_limit_bytes=2**20),
    )(*outs)


def solution(mesh):
    rows = P(("seq", "head"), None)
    return jax.shard_map(
        shards,
        mesh=mesh,
        in_specs=(rows, rows, rows, rows, P(), P()),
        out_specs=(rows, rows, rows, rows),
        check_vma=False,
    )
```
